128 devices in a mesh: tm: 8 (over z_lo, x), chan: 16 (over z_hi, y, core).
Axes of the slice: x: 4, y: 4, z: 4 (z_hi: 2, z_lo: 2; z = z_hi * 2 + z_lo), core: 2. Of those that a mesh axis runs over, the one named last changes fastest.
Arguments:
- record: bfloat16 [65536, 2048], P('tm', 'chan'), may hold values from -6 to 6
- starts: int32 [16], P('tm'), may hold values from 0 to 5192
Outputs:
- correlation: float32 [200, 2048, 128], P('tm', 'chan')
The draws below stay inside these ranges and needn't reach their ends.
Inputs may be any that keep to these rules, and one draw needn't show every extreme that they name: `starts`: each window lies inside its own group's 8192 samples.
All inputs are finite; a program needn't handle non-finite values.
Results may differ from the reference program's by a relative error of at most 0.0071.
Values may be sent and summed in bfloat16 or wider, within the bound.
A program may use at most 256 MiB of HBM per device.

```python
import math
import jax
import jax.numpy as jnp
from jax import lax

SAMP = 3000
F = 1501
BAND = 200
LAGS = 128
W_DEV = 2
SEG = 8192
CHANNELS = 2048
WINDOWS = 16
RECORD = 65536


def plant(values, stream_key, smallest, high):
    dims = values.shape
    spot = [jax.random.randint(jax.random.fold_in(stream_key, axis), (), 0, dims[axis]) for axis in range(len(dims))]
    values = values.at[tuple(spot)].set(smallest)
    longest = dims.index(max(dims))
    spot[longest] = (spot[longest] + 1) % dims[longest]
    return values.at[tuple(spot)].set(high)


def steps_of(rng, dims, pieces, low, high):
    loudness, own = 1.0, jax.random.fold_in(rng, 6)
    for dim, blocks in pieces:
        steps = jnp.exp(jax.random.uniform(jax.random.fold_in(own, dim), (blocks,), jnp.float32, low / len(pieces), high / len(pieces)))
        loudness = loudness * jnp.repeat(steps, dims[dim] // blocks).reshape([-1 if axis == dim else 1 for axis in range(len(dims))])
    return loudness


def bell_draw(own_key, dims, spread, reach, cuts=(), held_as=jnp.bfloat16):
    result = spread * jax.random.normal(own_key, dims, jnp.float32)
    if cuts:
        result = result * steps_of(own_key, dims, cuts, -0.22, 0.18)
    return jnp.clip(result, -reach, reach).astype(held_as)


def setup_inputs(seed: int = 0) -> dict:
    key_list = jax.random.split(jax.random.key(seed), 3)
    return {
        "record": bell_draw(key_list[0], (RECORD, CHANNELS), 1.0, 6.0, ((0, 8), (1, 16))),
        "starts": plant(jax.random.randint(key_list[1], (WINDOWS,), 0, SEG - SAMP + 1), jax.random.fold_in(key_list[1], 1), 0, SEG - SAMP).astype(jnp.int32),
    }


def dft_rows(rows):
    freq = jnp.arange(rows, dtype=jnp.int32)
    times = jnp.arange(SAMP, dtype=jnp.int32)
    phase = freq[:, None] * times[None, :] % SAMP
    angle = phase.astype(jnp.float32) * jnp.float32(2.0 * math.pi / SAMP)
    factor = (freq < F).astype(jnp.float32)[:, None] * jnp.float32(1.0 / math.sqrt(SAMP))
    return jnp.concatenate([jnp.cos(angle) * factor, -jnp.sin(angle) * factor], axis=0).astype(jnp.bfloat16)

def lag_rows(rows, windows):
    freq = jnp.arange(rows, dtype=jnp.int32)
    moved = jnp.arange(LAGS, dtype=jnp.int32) - LAGS // 2 + SAMP
    phase = freq[:, None] * moved[None, :] % SAMP
    angle = phase.astype(jnp.float32) * jnp.float32(2.0 * math.pi / SAMP)
    weight = jnp.where((freq == 0) | (freq == SAMP // 2), jnp.float32(1.0), jnp.float32(2.0))
    weight = weight * (freq < F).astype(jnp.float32)
    factor = weight[:, None] * jnp.float32(1.0 / math.sqrt(SAMP * windows))
    return jnp.stack([jnp.cos(angle) * factor, -jnp.sin(angle) * factor]).astype(jnp.bfloat16)

def whiten(spec):
    parts = spec.reshape(2, spec.shape[0] // 2, spec.shape[1])
    power = parts[0] * parts[0] + parts[1] * parts[1]
    padded = jnp.pad(power, ((1, 1), (0, 0)))
    smooth = (padded[:-2] + power + padded[2:]) / 3.0
    factor = 1.0 / jnp.maximum(jnp.sqrt(smooth), 0.5)
    return (parts * factor[None]).astype(jnp.bfloat16)

def conj_sum(own, partner):
    real_own = own[..., 0, :, :].astype(jnp.float32)
    imag_own = own[..., 1, :, :].astype(jnp.float32)
    real_far = partner[..., 0, :, :].astype(jnp.float32)
    imag_far = partner[..., 1, :, :].astype(jnp.float32)
    real = lax.optimization_barrier(jnp.sum(real_own * real_far + imag_own * imag_far, axis=-3))
    imag = lax.optimization_barrier(jnp.sum(imag_own * real_far - real_own * imag_far, axis=-3))
    return jnp.stack([real, imag], axis=-3).astype(jnp.bfloat16)

def reference(record, starts):
    table = dft_rows(F)

    def one_window(index):
        group = index // W_DEV
        first = (group * SEG + starts[index]).astype(jnp.int32)
        samples = lax.dynamic_slice_in_dim(record, first, SAMP, 0)
        return whiten(jnp.dot(table, samples, preferred_element_type=jnp.float32))
    white = lax.map(one_window, jnp.arange(WINDOWS, dtype=jnp.int32))
    padded = jnp.pad(white, ((0, 0), (0, 0), (0, 0), (0, BAND)))
    lags = lag_rows(F, WINDOWS).astype(jnp.float32)

    def one_offset(offset):
        partner = lax.dynamic_slice_in_dim(padded, offset, CHANNELS, 3)
        cross = conj_sum(white, partner)
        return jnp.einsum('sfc,sft->ct', cross.astype(jnp.float32), lags, precision=lax.Precision.HIGHEST)
    return lax.map(one_offset, jnp.arange(1, BAND + 1, dtype=jnp.int32))
```

```python
import math

import jax
import jax.numpy as jnp
import ml_dtypes
import numpy as np
from jax import lax
from jax.experimental import pallas as pl
from jax.experimental.pallas import tpu as pltpu
from jax.sharding import PartitionSpec as P

SAMP = 3000
F = 1501
ROWS = 1504
BAND = 200
LAGS = 128
HALF = LAGS // 2
SEG = 64
SLOTS = 48
SPAN = 192
POINTS = 191
BINS = 96
BF16 = ml_dtypes.bfloat16


def turns(a, b, period):
    return 2.0 * math.pi * (np.outer(a, b) % period) / period


def dft_table():
    angle = turns(np.arange(F), np.arange(SAMP), SAMP)
    table = np.zeros((2, ROWS, SAMP), np.float32)
    table[0, :F] = np.cos(angle) / math.sqrt(SAMP)
    table[1, :F] = -np.sin(angle) / math.sqrt(SAMP)
    return table.reshape(2 * ROWS, SAMP).astype(BF16)


def inverse_table(rows):
    time = (np.arange(rows) - HALF) % SAMP
    weight = np.full(F, 2.0)
    weight[0] = weight[-1] = 1.0
    angle = turns(time, np.arange(F), SAMP)
    table = np.zeros((rows, 2, ROWS), np.float32)
    table[:, 0, :F] = weight * np.cos(angle) / math.sqrt(SAMP)
    table[:, 1, :F] = -weight * np.sin(angle) / math.sqrt(SAMP)
    return table.reshape(rows, 2 * ROWS).astype(BF16)


def segment_tables():
    angle = turns(np.arange(BINS), np.arange(SPAN), POINTS)
    full = np.concatenate([np.cos(angle), -np.sin(angle)]) / math.sqrt(POINTS)
    full[:, POINTS:] = 0.0
    high = full.astype(BF16)
    low = (full - high.astype(np.float64)).astype(BF16)
    return high, np.concatenate([high[:, :SEG], low[:, :SEG]], axis=1)


def lag_table(windows):
    angle = turns(np.arange(BINS), np.arange(LAGS), POINTS)
    weight = np.full((BINS, 1), 2.0)
    weight[0] = 1.0
    table = np.stack([weight * np.cos(angle), -weight * np.sin(angle)], axis=1)
    return (table / math.sqrt(SAMP * windows)).reshape(2 * BINS, LAGS).astype(BF16)


def whiten(spec):
    parts = spec.reshape(2, ROWS, spec.shape[1])
    power = parts[0] * parts[0] + parts[1] * parts[1]
    padded = jnp.pad(power, ((1, 1), (0, 0)))
    smooth = (padded[:-2] + power + padded[2:]) / 3.0
    factor = 1.0 / jnp.maximum(jnp.sqrt(smooth), 0.5)
    return (parts * factor[None]).astype(jnp.bfloat16)


FIRST = 7
OUT_ROWS = FIRST + BAND + 8


def pair_kernel(ya, yd, fa, fd, lag, out, sega, bins, gram, rows):
    width = yd.shape[2] // 2

    def long_segment(s, carry):
        block = ya[pl.ds(pl.multiple_of(s * SEG, SEG), SPAN), :]
        spec = jnp.dot(fa[...], block, preferred_element_type=jnp.float32)
        bins[0, pl.ds(s, 2 * BINS, stride=SLOTS), :] = spec[:, :width]
        bins[1, pl.ds(s, 2 * BINS, stride=SLOTS), :] = spec[:, width:]
        return carry

    lax.fori_loop(0, SLOTS - 1, long_segment, 0)
    zero = jnp.zeros((2 * BINS, width), jnp.float32)
    bins[0, pl.ds(SLOTS - 1, 2 * BINS, stride=SLOTS), :] = zero
    bins[1, pl.ds(SLOTS - 1, 2 * BINS, stride=SLOTS), :] = zero

    def of_bin(b):
        real = pl.ds(pl.multiple_of(b * SLOTS, SLOTS), SLOTS)
        imag = pl.ds(pl.multiple_of((b + BINS) * SLOTS, SLOTS), SLOTS)
        return [bins[0, real, :], bins[1, real, :], bins[0, imag, :], bins[1, imag, :]]

    def turn_bin(b, carry):
        r0, r1, i0, i1 = of_bin(b)
        sega[b, :width, :] = jnp.concatenate([r0, r1, i0, i1], 0).T.astype(jnp.bfloat16)
        sega[b, width:, :] = jnp.concatenate([i0, i1, -r0, -r1], 0).T.astype(jnp.bfloat16)
        return carry

    lax.fori_loop(0, BINS, turn_bin, 0)

    for q in range(yd.shape[0]):

        def short_segment(s, carry):
            block = yd[q, pl.ds(pl.multiple_of(s * SEG, SEG), SEG), :]
            twice = jnp.concatenate([block, block], 0)
            spec = jnp.dot(fd[...], twice, preferred_element_type=jnp.float32)
            bins[0, pl.ds(s, 2 * BINS, stride=SLOTS), :] = spec[:, :width]
            bins[1, pl.ds(s, 2 * BINS, stride=SLOTS), :] = spec[:, width:]
            return carry

        lax.fori_loop(0, SLOTS, short_segment, 0)

        def one_bin(b, carry):
            far = jnp.concatenate(of_bin(b), 0).astype(jnp.bfloat16)
            cross = jnp.dot(sega[b], far, preferred_element_type=jnp.float32)
            gram[pl.ds(pl.multiple_of(b * 2 * width, 2 * width), 2 * width), :] = cross
            return carry

        lax.fori_loop(0, BINS, one_bin, 0)

        def one_channel(c, carry):
            cross = gram[pl.ds(c, 2 * BINS, stride=width), :].astype(jnp.bfloat16)
            lags = lax.dot_general(
                cross, lag[...], (((0,), (0,)), ((), ())), preferred_element_type=jnp.float32
            )
            for i in range(width // 8):
                k = q * width + 8 * i - c

                @pl.when((k > -8) & (k <= BAND))
                def _():
                    first = (k + FIRST) * width + c
                    rows[pl.ds(first, 8, stride=width), :] = lags[8 * i : 8 * i + 8]

            return carry

        lax.fori_loop(0, width, one_channel, 0)

    def finish(k, carry):
        first = pl.multiple_of((k + FIRST + 1) * width, width)
        out[k] = rows[pl.ds(first, width), :].astype(jnp.bfloat16)
        return carry

    lax.fori_loop(0, BAND, finish, 0)


def correlate(ya, yd, windows):
    width = yd.shape[2] // 2
    fa, fd = segment_tables()
    vmem = pl.BlockSpec(memory_space=pltpu.VMEM)
    return pl.pallas_call(
        pair_kernel,
        out_shape=jax.ShapeDtypeStruct((BAND, width, LAGS), jnp.bfloat16),
        in_specs=[vmem] * 5,
        out_specs=vmem,
        scratch_shapes=[
            pltpu.VMEM((BINS, 2 * width, 4 * SLOTS), jnp.bfloat16),
            pltpu.VMEM((2, 2 * BINS * SLOTS, width), jnp.float32),
            pltpu.VMEM((2 * BINS * width, width), jnp.float32),
            pltpu.VMEM((OUT_ROWS * width, LAGS), jnp.float32),
        ],
        compiler_params=pltpu.CompilerParams(vmem_limit_bytes=62 * 2**20),
        cost_estimate=pl.CostEstimate(flops=6 * 10**9, bytes_accessed=20 * 10**6, transcendentals=0),
    )(ya, yd, jnp.asarray(fa), jnp.asarray(fd), jnp.asarray(lag_table(windows)))


def time_series(record, starts):
    samples = jnp.concatenate(
        [lax.dynamic_slice_in_dim(record, starts[w], SAMP, 0) for w in range(starts.shape[0])], 1
    )
    spec = jnp.dot(jnp.asarray(dft_table()), samples, preferred_element_type=jnp.float32)
    white = whiten(spec).reshape(2 * ROWS, samples.shape[1])
    table = jnp.asarray(inverse_table(SEG * (SLOTS + 2)))
    return jnp.dot(table, white, preferred_element_type=jnp.float32).astype(jnp.bfloat16)


def body(record, starts):
    groups = lax.axis_size("tm")
    blocks = lax.axis_size("chan")
    ya = time_series(record, starts)
    own = jnp.pad(ya[HALF : HALF + SAMP], ((0, SEG * SLOTS - SAMP), (0, 0)))
    after = lax.ppermute(own, "chan", [(j, j - 1) for j in range(1, blocks)])
    beyond = lax.ppermute(own, "chan", [(j, j - 2) for j in range(2, blocks)])
    yd = jnp.stack([own, after, beyond])
    part = correlate(ya, yd, starts.shape[0] * groups)
    total = lax.psum_scatter(part, "tm", scatter_dimension=0, tiled=True)
    return total.astype(jnp.float32)


def solution(mesh):
    return jax.shard_map(
        body,
        mesh=mesh,
        in_specs=(P("tm", "chan"), P("tm")),
        out_specs=P("tm", "chan", None),
        check_vma=False,
    )
```

```python
import math

import jax
import jax.numpy as jnp
import ml_dtypes
import numpy as np
from jax import lax
from jax.experimental import pallas as pl
from jax.experimental.pallas import tpu as pltpu
from jax.sharding import PartitionSpec as P

SAMP = 3000
F = 1501
ROWS = 1504
BAND = 200
LAGS = 128
HALF = LAGS // 2
SEG = 64
SLOTS = 48
SPAN = 192
POINTS = 191
BINS = 96
BF16 = ml_dtypes.bfloat16


def turns(a, b, period):
    return 2.0 * math.pi * (np.outer(a, b) % period) / period


def dft_table():
    angle = turns(np.arange(F), np.arange(SAMP), SAMP)
    table = np.zeros((2, ROWS, SAMP), np.float32)
    table[0, :F] = np.cos(angle) / math.sqrt(SAMP)
    table[1, :F] = -np.sin(angle) / math.sqrt(SAMP)
    return table.reshape(2 * ROWS, SAMP).astype(BF16)


def inverse_table(rows):
    time = (np.arange(rows) - HALF) % SAMP
    weight = np.full(F, 2.0)
    weight[0] = weight[-1] = 1.0
    angle = turns(time, np.arange(F), SAMP)
    table = np.zeros((rows, 2, ROWS), np.float32)
    table[:, 0, :F] = weight * np.cos(angle) / math.sqrt(SAMP)
    table[:, 1, :F] = -weight * np.sin(angle) / math.sqrt(SAMP)
    return table.reshape(rows, 2 * ROWS).astype(BF16)


def segment_tables():
    angle = turns(np.arange(BINS), np.arange(SPAN), POINTS)
    full = np.stack([np.cos(angle), -np.sin(angle)], axis=1) / math.sqrt(POINTS)
    full = full.reshape(2 * BINS, SPAN)
    full[:, POINTS:] = 0.0
    high = full.astype(BF16)
    low = (full - high.astype(np.float64)).astype(BF16)
    return high, np.concatenate([high[:, :SEG], low[:, :SEG]], axis=1)


def lag_table(windows):
    angle = turns(np.arange(BINS), np.arange(LAGS), POINTS)
    weight = np.full((BINS, 1), 2.0)
    weight[0] = 1.0
    table = np.stack([weight * np.cos(angle), -weight * np.sin(angle)], axis=1)
    return (table / math.sqrt(SAMP * windows)).reshape(2 * BINS, LAGS).astype(BF16)


def whiten(spec):
    parts = spec.reshape(2, ROWS, spec.shape[1])
    power = parts[0] * parts[0] + parts[1] * parts[1]
    padded = jnp.pad(power, ((1, 1), (0, 0)))
    smooth = (padded[:-2] + power + padded[2:]) / 3.0
    factor = 1.0 / jnp.maximum(jnp.sqrt(smooth), 0.5)
    return (parts * factor[None]).astype(jnp.bfloat16)


FIRST = 8
OUT_ROWS = FIRST + BAND + 9
HELD = 2 * 2 * SLOTS
CHUNK = 16
RING = 4
LIVE = 4
MESH = pl.DeviceIdType.MESH


def unrolled(count, step, times):
    def several(i, carry):
        step([i * times + u for u in range(times)])
        return carry

    lax.fori_loop(0, count // times, several, 0)


def pair_kernel(
    ya, own, fa, fd, lag, out,
    sega, bins, gram, rows, near, far, part, hop, land, across,
    sent, come, sent_y, come_y,
):
    width = own.shape[1] // 2
    share = out.shape[0]
    chunks = width // CHUNK
    blocks = lax.axis_size("chan")
    i, j = lax.axis_index("tm"), lax.axis_index("chan")
    x, z = lax.rem(i, RING), i // RING
    right = {"tm": z * RING + lax.rem(x + 1, RING)}
    left = {"tm": z * RING + lax.rem(x + RING - 1, RING)}
    other = {"tm": (1 - z) * RING + x}
    odd = lax.rem(j, 2) == 1

    def behind(distance):
        return {"chan": lax.rem(j + blocks + distance, blocks)}

    barrier = pltpu.get_barrier_semaphore()
    peers = (right, left, other, behind(-1), behind(1), behind(-2), behind(2))
    for device in peers:
        pl.semaphore_signal(barrier, inc=1, device_id=device, device_id_type=MESH)
    pl.semaphore_wait(barrier, len(peers))

    def remote(source, target, send, receive, device):
        return pltpu.make_async_remote_copy(
            src_ref=source, dst_ref=target, send_sem=send, recv_sem=receive,
            device_id=device, device_id_type=MESH,
        )

    to_near = remote(own, near, sent_y.at[0], come_y.at[0], behind(-1))
    to_far = remote(own, far, sent_y.at[1], come_y.at[1], behind(-2))
    pass_on = remote(near, far, sent_y.at[2], come_y.at[1], behind(-1))
    to_near.start()

    @pl.when(odd)
    def _():
        to_far.start()

    def spread(slot, s, spec):
        at = slot * 2 * SLOTS + s
        bins[pl.ds(at, 2 * BINS, stride=HELD), :] = spec[:, :width]
        bins[pl.ds(at + SLOTS, 2 * BINS, stride=HELD), :] = spec[:, width:]

    def long_segments(index):
        specs = []
        for s in index:
            block = ya[pl.ds(pl.multiple_of(s * SEG, SEG), SPAN), :]
            specs.append(jnp.dot(fa[...], block, preferred_element_type=jnp.float32))
        for s, spec in zip(index, specs):
            spread(0, s, spec)

    def short_segments(source, slot, holds):
        table = fd[...]
        if holds is not None:
            table = jnp.where(holds, table, jnp.zeros_like(table))

        def step(index):
            specs = []
            for s in index:
                block = source[pl.ds(pl.multiple_of(s * SEG, SEG), SEG), :]
                twice = jnp.concatenate([block, block], 0)
                specs.append(jnp.dot(table, twice, preferred_element_type=jnp.float32))
            for s, spec in zip(index, specs):
                spread(slot, s, spec)

        unrolled(SLOTS, step, 8)

    def of_bin(slot, b):
        first = pl.multiple_of(b * 2 * HELD, 2 * HELD) + slot * 2 * SLOTS
        return bins[pl.ds(first, 2 * SLOTS), :], bins[pl.ds(first + HELD, 2 * SLOTS), :]

    def turn_bins(index):
        for b in index:
            sega[b] = jnp.concatenate(of_bin(0, b), 0).T.astype(jnp.bfloat16)

    def product(slot, b):
        real, imag = [part.astype(jnp.bfloat16) for part in of_bin(slot, b)]
        both = jnp.concatenate(
            [jnp.concatenate([real, imag], 0), jnp.concatenate([-imag, real], 0)], 1
        )
        return jnp.dot(sega[b], both, preferred_element_type=jnp.float32)

    def keep(target, pitch, b, cross):
        first = pl.multiple_of(b * 2 * pitch, 2 * pitch)
        target[pl.ds(first, width), :] = cross[:, :width]
        target[pl.ds(first + pitch, width), :] = cross[:, width:]

    def gram_next(index):
        for b, cross in zip(index, [product(1, b) for b in index]):
            keep(gram, width, b, cross)

    same = lax.broadcasted_iota(jnp.int32, (width, 2 * width), 1) % width
    same = same > lax.broadcasted_iota(jnp.int32, (width, 2 * width), 0)

    def gram_own(index):
        crosses = [jnp.where(same, product(0, b), product(1, b)) for b in index]
        for b, cross in zip(index, crosses):
            keep(bins, HELD, b, cross)

    def place_next(ahead, c):
        return width + ahead - c

    def place_own(ahead, c):
        return jnp.where(ahead + 7 > c, ahead - c, 2 * width + ahead - c)

    def lag_step(source, pitch, place, base):
        def step(index):
            cross = jnp.concatenate(
                [
                    source[pl.ds(base + c, 2 * BINS, stride=pitch), :].astype(jnp.bfloat16)
                    for c in index
                ],
                1,
            )
            lags = lax.dot_general(
                cross, lag[...], (((0,), (0,)), ((), ())), preferred_element_type=jnp.float32
            )
            for u, c in enumerate(index):
                for e in range(width // 8):
                    k = jnp.clip(place(8 * e, base + c), -FIRST, BAND + 1)
                    at = u * width + 8 * e
                    rows[pl.ds((k + FIRST) * CHUNK + c, 8, stride=CHUNK), :] = lags[at : at + 8]

        return step

    unrolled(SLOTS, long_segments, 8)
    unrolled(BINS, turn_bins, 8)
    short_segments(own, 0, None)
    to_near.wait_recv()

    @pl.when(odd)
    def _():
        pass_on.start()

    short_segments(near, 1, j < blocks - 1)
    unrolled(BINS, gram_next, 8)
    to_far.wait_recv()
    short_segments(far, 1, j < blocks - 2)
    unrolled(BINS, gram_own, 8)

    def at(column, row):
        return row * RING + lax.rem(column + RING, RING)

    def message(n, m):
        slot = n % LIVE
        source, target, device = [
            (part.at[slot, at(x + 2, 0)], hop.at[n, 0], right),
            (part.at[slot, at(x + 2, 1)], hop.at[n, 1], left),
            (part.at[slot, at(x + 1, 1)], land.at[n, 0, 1], right),
            (part.at[slot, at(x - 1, 0)], land.at[n, 1, 0], left),
            (part.at[slot, at(x + 1, 0)], land.at[n, 0, 0], right),
            (part.at[slot, at(x - 1, 1)], land.at[n, 1, 1], left),
            (part.at[slot, at(x, 1 - z)], across.at[n], other),
        ][m]
        return remote(source, target, sent.at[n, m], come.at[n, m], device)

    def plus(n, place, others):
        slot = n % LIVE

        def step(k, carry):
            total = part[slot, place, k].astype(jnp.float32)
            for ref in others:
                total += ref[k].astype(jnp.float32)
            part[slot, place, k] = total.astype(jnp.bfloat16)
            return carry

        lax.fori_loop(0, share, step, 0)

    def begin(n):
        unrolled(CHUNK, lag_step(gram, width, place_next, n * CHUNK), 8)
        unrolled(CHUNK, lag_step(bins, HELD, place_own, n * CHUNK), 8)
        slot = n % LIVE

        def step(k, carry):
            for d in range(BAND // share):
                first = pl.multiple_of((d * share + k + FIRST + 1) * CHUNK, CHUNK)
                part[slot, d, k] = rows[pl.ds(first, CHUNK), :].astype(jnp.bfloat16)
            return carry

        lax.fori_loop(0, share, step, 0)
        for m in range(4):
            message(n, m).start()

    def second(n):
        for m in range(2):
            message(n, m).wait_recv()
        plus(n, at(x + 1, 0), [hop.at[n, 0]])
        message(n, 4).start()
        plus(n, at(x - 1, 1), [hop.at[n, 1]])
        message(n, 5).start()

    def third(n):
        for m in range(2, 6):
            message(n, m).wait_recv()
        plus(n, at(x, 1 - z), [land.at[n, 0, 1 - z], land.at[n, 1, 1 - z]])
        message(n, 6).start()

    def last(n):
        message(n, 6).wait_recv()
        slot = n % LIVE

        def step(k, carry):
            total = part[slot, at(x, z), k].astype(jnp.float32)
            for ref in (land.at[n, 0, z], land.at[n, 1, z], across.at[n]):
                total += ref[k].astype(jnp.float32)
            out[k, n * CHUNK : (n + 1) * CHUNK, :] = total
            return carry

        lax.fori_loop(0, share, step, 0)
        for m in range(7):
            message(n, m).wait_send()

    for n in range(chunks + 3):
        for late, stage in enumerate((begin, second, third, last)):
            if 0 <= n - late < chunks:
                stage(n - late)

    to_near.wait_send()

    @pl.when(odd)
    def _():
        to_far.wait_send()
        pass_on.wait_send()


def correlate(ya, own, windows, groups):
    width = own.shape[1] // 2
    share = BAND // groups
    chunks = width // CHUNK
    fa, fd = segment_tables()
    vmem = pl.BlockSpec(memory_space=pltpu.VMEM)
    block = (share, CHUNK, LAGS)
    return pl.pallas_call(
        pair_kernel,
        out_shape=jax.ShapeDtypeStruct((share, width, LAGS), jnp.float32),
        in_specs=[vmem] * 5,
        out_specs=vmem,
        scratch_shapes=[
            pltpu.VMEM((BINS, width, HELD), jnp.bfloat16),
            pltpu.VMEM((2 * BINS * HELD, width), jnp.float32),
            pltpu.VMEM((2 * BINS * width, width), jnp.float32),
            pltpu.VMEM((OUT_ROWS * CHUNK, LAGS), jnp.float32),
            pltpu.VMEM(own.shape, jnp.bfloat16),
            pltpu.VMEM(own.shape, jnp.bfloat16),
            pltpu.VMEM((LIVE, groups) + block, jnp.bfloat16),
            pltpu.VMEM((chunks, 2) + block, jnp.bfloat16),
            pltpu.VMEM((chunks, 2, 2) + block, jnp.bfloat16),
            pltpu.VMEM((chunks,) + block, jnp.bfloat16),
            pltpu.SemaphoreType.DMA((chunks, 7)),
            pltpu.SemaphoreType.DMA((chunks, 7)),
            pltpu.SemaphoreType.DMA((3,)),
            pltpu.SemaphoreType.DMA((2,)),
        ],
        compiler_params=pltpu.CompilerParams(
            vmem_limit_bytes=62 * 2**20, collective_id=0, has_side_effects=True
        ),
        cost_estimate=pl.CostEstimate(flops=6 * 10**9, bytes_accessed=20 * 10**6, transcendentals=0),
    )(ya, own, jnp.asarray(fa), jnp.asarray(fd), jnp.asarray(lag_table(windows)))


def time_series(record, starts):
    samples = jnp.concatenate(
        [lax.dynamic_slice_in_dim(record, starts[w], SAMP, 0) for w in range(starts.shape[0])], 1
    )
    spec = jnp.dot(jnp.asarray(dft_table()), samples, preferred_element_type=jnp.float32)
    white = whiten(spec).reshape(2 * ROWS, samples.shape[1])
    table = jnp.asarray(inverse_table(SEG * (SLOTS + 2)))
    return jnp.dot(table, white, preferred_element_type=jnp.float32).astype(jnp.bfloat16)


def body(record, starts):
    groups = lax.axis_size("tm")
    ya = time_series(record, starts)
    own = jnp.pad(ya[HALF : HALF + SAMP], ((0, SEG * SLOTS - SAMP), (0, 0)))
    return correlate(ya, own, starts.shape[0] * groups, groups)


def solution(mesh):
    return jax.shard_map(
        body,
        mesh=mesh,
        in_specs=(P("tm", "chan"), P("tm")),
        out_specs=P("tm", "chan", None),
        check_vma=False,
    )
```

```python
import math

import jax
import jax.numpy as jnp
import ml_dtypes
import numpy as np
from jax import lax
from jax.experimental import pallas as pl
from jax.experimental.pallas import tpu as pltpu
from jax.sharding import PartitionSpec as P

SAMP = 3000
F = 1501
ROWS = 1504
BAND = 200
LAGS = 128
HALF = LAGS // 2
SEG = 64
SLOTS = 48
SPAN = 192
POINTS = 191
BINS = 96
BF16 = ml_dtypes.bfloat16


def turns(a, b, period):
    return 2.0 * math.pi * (np.outer(a, b) % period) / period


def dft_table():
    angle = turns(np.arange(F), np.arange(SAMP), SAMP)
    table = np.zeros((2, ROWS, SAMP), np.float32)
    table[0, :F] = np.cos(angle) / math.sqrt(SAMP)
    table[1, :F] = -np.sin(angle) / math.sqrt(SAMP)
    return table.reshape(2 * ROWS, SAMP).astype(BF16)


def inverse_table(rows):
    time = (np.arange(rows) - HALF) % SAMP
    weight = np.full(F, 2.0)
    weight[0] = weight[-1] = 1.0
    angle = turns(time, np.arange(F), SAMP)
    table = np.zeros((rows, 2, ROWS), np.float32)
    table[:, 0, :F] = weight * np.cos(angle) / math.sqrt(SAMP)
    table[:, 1, :F] = -weight * np.sin(angle) / math.sqrt(SAMP)
    return table.reshape(rows, 2 * ROWS).astype(BF16)


def segment_tables():
    angle = turns(np.arange(BINS), np.arange(SPAN), POINTS)
    full = np.stack([np.cos(angle), -np.sin(angle)], axis=1) / math.sqrt(POINTS)
    full = full.reshape(2 * BINS, SPAN)
    full[:, POINTS:] = 0.0
    high = full.astype(BF16)
    low = (full - high.astype(np.float64)).astype(BF16)
    return high, np.concatenate([high[:, :SEG], low[:, :SEG]], axis=1)


def lag_table(windows):
    angle = turns(np.arange(BINS), np.arange(LAGS), POINTS)
    weight = np.full((BINS, 1), 2.0)
    weight[0] = 1.0
    table = np.stack([weight * np.cos(angle), -weight * np.sin(angle)], axis=1)
    return (table / math.sqrt(SAMP * windows)).reshape(2 * BINS, LAGS).astype(BF16)


def whiten(spec):
    parts = spec.reshape(2, ROWS, spec.shape[1])
    power = parts[0] * parts[0] + parts[1] * parts[1]
    padded = jnp.pad(power, ((1, 1), (0, 0)))
    smooth = (padded[:-2] + power + padded[2:]) / 3.0
    factor = 1.0 / jnp.maximum(jnp.sqrt(smooth), 0.5)
    return (parts * factor[None]).astype(jnp.bfloat16)


FIRST = 8
OUT_ROWS = FIRST + BAND + 9
HELD = 2 * 2 * SLOTS
CHUNK = 16
RING = 4
PARTS = 3
BIN_PITCH = 225
NEXT_PITCH = 129
ROW_PITCH = 17
SECOND = 128
NO_FAR = 48
KINDS = "XZXXZXZX"
STEPS = (
    "b0", "b1", "s0", "b2", "f", "s1", "s2", "t0", "t1", "b3", "t2",
    "b4", "b5", "s3", "b6", "s5", "b7", "s4", "t3", "l0", "l1", "t5",
    "l2", "s7", "t4", "s6", "l3", "t7", "l4", "l5", "t6", "l7", "l6",
)
MESH = pl.DeviceIdType.MESH


def unrolled(count, step, times):
    def several(i, carry):
        step([i * times + u for u in range(times)])
        return carry

    lax.fori_loop(0, count // times, several, 0)


def pair_kernel(
    ya, own, fa, fd, lag, out,
    sega, bins, gram, rows, near, far, part, inbox,
    sent, come, sent_y, come_y,
):
    width = own.shape[1] // 2
    share = out.shape[0]
    blocks = lax.axis_size("chan")
    i, j = lax.axis_index("tm"), lax.axis_index("chan")
    x, z = lax.rem(i, RING), i // RING
    right = {"tm": z * RING + lax.rem(x + 1, RING)}
    left = {"tm": z * RING + lax.rem(x + RING - 1, RING)}
    other = {"tm": (1 - z) * RING + x}
    odd = lax.rem(j, 2) == 1

    def behind(distance):
        return {"chan": lax.rem(j + blocks + distance, blocks)}

    barrier = pltpu.get_barrier_semaphore()
    peers = (right, left, other, behind(-1), behind(1), behind(-2), behind(2))
    for device in peers:
        pl.semaphore_signal(barrier, inc=1, device_id=device, device_id_type=MESH)
    pl.semaphore_wait(barrier, len(peers))

    def remote(source, target, send, receive, device):
        return pltpu.make_async_remote_copy(
            src_ref=source, dst_ref=target, send_sem=send, recv_sem=receive,
            device_id=device, device_id_type=MESH,
        )

    length = SLOTS // PARTS * SEG
    to_near = []
    for p in range(PARTS):
        piece = pl.ds(p * length, length)
        to_near.append(
            remote(own.at[piece], near.at[piece], sent_y.at[p], come_y.at[p], behind(-1))
        )
    to_far = remote(own, far, sent_y.at[PARTS], come_y.at[PARTS], behind(-2))
    pass_on = remote(near, far, sent_y.at[PARTS + 1], come_y.at[PARTS], behind(-1))
    for piece in to_near:
        piece.start()

    def spread(slot, s, spec):
        at = slot * SECOND + s
        bins[pl.ds(at, 2 * BINS, stride=BIN_PITCH), :] = spec[:, :width]
        bins[pl.ds(at + SLOTS, 2 * BINS, stride=BIN_PITCH), :] = spec[:, width:]

    def long_segments(index):
        specs = []
        for s in index:
            block = ya[pl.ds(pl.multiple_of(s * SEG, SEG), SPAN), :]
            specs.append(jnp.dot(fa[...], block, preferred_element_type=jnp.float32))
        for s, spec in zip(index, specs):
            spread(0, s, spec)

    def short_segments(source, slot, absent, first, count):
        def step(index):
            specs = []
            for s in index:
                block = source[pl.ds(pl.multiple_of((first + s) * SEG, SEG), SEG), :]
                twice = jnp.concatenate([block, block], 0)
                specs.append(jnp.dot(fd[absent], twice, preferred_element_type=jnp.float32))
            for s, spec in zip(index, specs):
                spread(slot, first + s, spec)

        unrolled(count, step, 8)

    def of_bin(slot, b):
        first = b * 2 * BIN_PITCH + slot * SECOND
        return bins[pl.ds(first, 2 * SLOTS), :], bins[pl.ds(first + BIN_PITCH, 2 * SLOTS), :]

    def turn_bins(index):
        for b in index:
            sega[b] = jnp.concatenate(of_bin(0, b), 0).astype(jnp.bfloat16).T

    def product(slot, b, first):
        real, imag = [part.astype(jnp.bfloat16) for part in of_bin(slot, b)]
        both = jnp.concatenate(
            [jnp.concatenate([real, imag], 0), jnp.concatenate([-imag, real], 0)], 1
        )
        return jnp.dot(sega[b, first:, :], both, preferred_element_type=jnp.float32)

    def keep(target, pitch, b, cross):
        first = b * 2 * pitch
        target[pl.ds(first, width), :] = cross[:, :width]
        target[pl.ds(first + pitch, width), :] = cross[:, width:]

    def gram_next(index):
        for b, cross in zip(index, [product(1, b, 0) for b in index]):
            keep(gram, NEXT_PITCH, b, cross)

    def gram_own(index):
        for b, cross in zip(index, [product(0, b, 0) for b in index]):
            keep(bins, BIN_PITCH, b, cross)

    tall = width - NO_FAR
    same = lax.broadcasted_iota(jnp.int32, (tall, width), 1)
    same = same > lax.broadcasted_iota(jnp.int32, (tall, width), 0) + NO_FAR

    def gram_far(index):
        crosses = [product(1, b, NO_FAR) for b in index]
        places = [pl.ds((2 * b + h) * BIN_PITCH + NO_FAR, tall) for b in index for h in range(2)]
        before = [bins[place, :] for place in places]
        for e, place in enumerate(places):
            h = e % 2
            cross = crosses[e // 2][:, h * width : (h + 1) * width]
            bins[place, :] = jnp.where(same, before[e], cross)

    def place_next(ahead, c):
        return width + ahead - c

    def place_own(ahead, c):
        return jnp.where(ahead + 7 > c, ahead - c, 2 * width + ahead - c)

    def lag_step(source, pitch, place, base):
        def step(index):
            cross = jnp.concatenate(
                [
                    source[pl.ds(base + c, 2 * BINS, stride=pitch), :].astype(jnp.bfloat16)
                    for c in index
                ],
                1,
            )
            lags = lax.dot_general(
                cross, lag[...], (((0,), (0,)), ((), ())), preferred_element_type=jnp.float32
            )
            for u, c in enumerate(index):
                for e in range(width // 8):
                    k = jnp.clip(place(8 * e, base + c), -FIRST, BAND + 1)
                    at = u * width + 8 * e
                    first = (k + FIRST) * ROW_PITCH + c
                    rows[pl.ds(first, 8, stride=ROW_PITCH), :] = lags[at : at + 8]

        return step

    unrolled(SLOTS, long_segments, 8)
    unrolled(BINS, turn_bins, 8)
    short_segments(own, 0, 0, 0, SLOTS)

    @pl.when(odd)
    def _():
        to_far.start()

    unrolled(BINS, gram_own, 8)
    near_absent = jnp.where(j < blocks - 1, 0, 1)
    for p in range(PARTS):
        to_near[p].wait_recv()
        short_segments(near, 1, near_absent, p * (SLOTS // PARTS), SLOTS // PARTS)

    @pl.when(odd)
    def _():
        pass_on.start()

    unrolled(BINS, gram_next, 8)

    def take_far():
        to_far.wait_recv()
        short_segments(far, 1, jnp.where(j < blocks - 2, 0, 1), 0, SLOTS)
        unrolled(BINS, gram_far, 8)

    def at(column, row):
        return row * RING + lax.rem(column + RING, RING)

    half = share // 2 + 1
    low, high, whole = (0, half), (half, share - half), (0, share)

    def message(n, m):
        def block(column, row, ks):
            return part.at[n, at(column, row), pl.ds(*ks)]

        def box(place, ks):
            return inbox.at[n, place, pl.ds(*ks)]

        if KINDS[n] == "X":
            source, target, device = [
                (block(x + 2, 0, whole), box(0, whole), right),
                (block(x + 2, 1, whole), box(1, whole), left),
                (block(x + 1, 1, whole), box(3, whole), right),
                (block(x - 1, 0, whole), box(4, whole), left),
                (block(x + 1, 0, whole), box(2, whole), right),
                (block(x - 1, 1, whole), box(5, whole), left),
                (block(x, 1 - z, whole), box(6, whole), other),
            ][m]
        else:
            source, target, device = [
                (part.at[n, pl.ds((1 - z) * RING, RING)], inbox.at[n, pl.ds(0, RING)], other),
                (block(x + 2, z, low), box(4, low), right),
                (block(x + 2, z, high), box(4, high), left),
                (block(x + 1, z, high), box(5, high), right),
                (block(x - 1, z, low), box(6, low), left),
                (block(x + 1, z, low), box(5, low), right),
                (block(x - 1, z, high), box(6, high), left),
            ][m]
        return remote(source, target, sent.at[n, m], come.at[n, m], device)

    def start(n, *which):
        for m in which:
            message(n, m).start()

    def wait(n, *which):
        for m in which:
            message(n, m).wait_recv()

    def plus(n, place, boxes, ks):
        first, count = ks

        def step(index):
            for k in index:
                total = part[n, place, first + k].astype(jnp.float32)
                for box in boxes:
                    total += inbox[n, box, first + k].astype(jnp.float32)
                part[n, place, first + k] = total.astype(jnp.bfloat16)

        unrolled(count, step, 5 if count % 5 == 0 else count)

    def begin(n):
        unrolled(CHUNK, lag_step(gram, NEXT_PITCH, place_next, n * CHUNK), 8)
        unrolled(CHUNK, lag_step(bins, BIN_PITCH, place_own, n * CHUNK), 8)

        def step(index):
            for k in index:
                for d in range(BAND // share):
                    first = (d * share + k + FIRST + 1) * ROW_PITCH
                    part[n, d, k] = rows[pl.ds(first, CHUNK), :].astype(jnp.bfloat16)

        unrolled(share, step, 5)
        start(n, *((0, 1, 2, 3) if KINDS[n] == "X" else (0,)))

    def second(n):
        if KINDS[n] == "X":
            wait(n, 0, 1)
            plus(n, at(x + 1, 0), [0], whole)
            start(n, 4)
            plus(n, at(x - 1, 1), [1], whole)
            start(n, 5)
        else:
            wait(n, 0)
            for step in (2, 1, 3, 0):
                plus(n, at(x + step, z), [(x + step) % RING], whole)
                start(n, *{2: (1, 2), 1: (3,), 3: (4,), 0: ()}[step])

    def third(n):
        if KINDS[n] == "X":
            wait(n, 2, 3, 4, 5)
            plus(n, at(x, 1 - z), [3 - z, 5 - z], whole)
            start(n, 6)
        else:
            wait(n, 1, 2)
            plus(n, at(x + 1, z), [4], low)
            start(n, 5)
            plus(n, at(x - 1, z), [4], high)
            start(n, 6)

    def last(n):
        if KINDS[n] == "X":
            wait(n, 6)
            boxes = (2 + z, 4 + z, 6)
        else:
            wait(n, 3, 4, 5, 6)
            boxes = (5, 6)

        def step(index):
            for k in index:
                total = part[n, at(x, z), k].astype(jnp.float32)
                for box in boxes:
                    total += inbox[n, box, k].astype(jnp.float32)
                out[k, n * CHUNK : (n + 1) * CHUNK, :] = total

        unrolled(share, step, 5)
        for m in range(7):
            message(n, m).wait_send()

    stages = {"b": begin, "s": second, "t": third, "l": last}
    for name in STEPS:
        if name == "f":
            take_far()
        else:
            stages[name[0]](int(name[1:]))

    for piece in to_near:
        piece.wait_send()

    @pl.when(odd)
    def _():
        to_far.wait_send()
        pass_on.wait_send()


def correlate(ya, own, windows, groups):
    width = own.shape[1] // 2
    share = BAND // groups
    chunks = width // CHUNK
    fa, fd = segment_tables()
    fd = np.stack([fd, np.zeros_like(fd)])
    vmem = pl.BlockSpec(memory_space=pltpu.VMEM)
    block = (share, CHUNK, LAGS)
    return pl.pallas_call(
        pair_kernel,
        out_shape=jax.ShapeDtypeStruct((share, width, LAGS), jnp.float32),
        in_specs=[vmem] * 5,
        out_specs=vmem,
        scratch_shapes=[
            pltpu.VMEM((BINS, width, HELD), jnp.bfloat16),
            pltpu.VMEM((2 * BINS * BIN_PITCH, width), jnp.float32),
            pltpu.VMEM((2 * BINS * NEXT_PITCH, width), jnp.float32),
            pltpu.VMEM((OUT_ROWS * ROW_PITCH, LAGS), jnp.float32),
            pltpu.VMEM(own.shape, jnp.bfloat16),
            pltpu.VMEM(own.shape, jnp.bfloat16),
            pltpu.VMEM((chunks, groups) + block, jnp.bfloat16),
            pltpu.VMEM((chunks, 7) + block, jnp.bfloat16),
            pltpu.SemaphoreType.DMA((chunks, 7)),
            pltpu.SemaphoreType.DMA((chunks, 7)),
            pltpu.SemaphoreType.DMA((PARTS + 2,)),
            pltpu.SemaphoreType.DMA((PARTS + 1,)),
        ],
        compiler_params=pltpu.CompilerParams(
            vmem_limit_bytes=62 * 2**20, collective_id=0, has_side_effects=True
        ),
        cost_estimate=pl.CostEstimate(flops=6 * 10**9, bytes_accessed=20 * 10**6, transcendentals=0),
    )(ya, own, jnp.asarray(fa), jnp.asarray(fd), jnp.asarray(lag_table(windows)))


def time_series(record, starts):
    samples = jnp.concatenate(
        [lax.dynamic_slice_in_dim(record, starts[w], SAMP, 0) for w in range(starts.shape[0])], 1
    )
    spec = jnp.dot(jnp.asarray(dft_table()), samples, preferred_element_type=jnp.float32)
    white = whiten(spec).reshape(2 * ROWS, samples.shape[1])
    table = jnp.asarray(inverse_table(SEG * (SLOTS + 2)))
    return jnp.dot(table, white, preferred_element_type=jnp.float32).astype(jnp.bfloat16)


def body(record, starts):
    groups = lax.axis_size("tm")
    ya = time_series(record, starts)
    own = jnp.pad(ya[HALF : HALF + SAMP], ((0, SEG * SLOTS - SAMP), (0, 0)))
    return correlate(ya, own, starts.shape[0] * groups, groups)


def solution(mesh):
    return jax.shard_map(
        body,
        mesh=mesh,
        in_specs=(P("tm", "chan"), P("tm")),
        out_specs=P("tm", "chan", None),
        check_vma=False,
    )
```

```python
import math

import jax
import jax.numpy as jnp
import ml_dtypes
import numpy as np
from jax import lax
from jax.experimental import pallas as pl
from jax.experimental.pallas import tpu as pltpu
from jax.sharding import PartitionSpec as P

SAMP = 3000
F = 1501
PAD = 3072
PIECE = 192
PIECES = 8
BAND = 200
LAGS = 128
HALF = LAGS // 2
SEG = 64
SLOTS = 48
FULL = SAMP // SEG
SPAN = 192
POINTS = 191
BINS = 96
SERIES = SEG * (SLOTS + 2)
BF16 = ml_dtypes.bfloat16


def turns(a, b, period):
    return 2.0 * math.pi * (np.outer(a, b) % period) / period


def by_pieces(real, imag):
    parts = np.zeros((2, PIECES * PIECE) + real.shape[1:], np.float32)
    parts[0, :F], parts[1, :F] = real, imag
    parts = parts.reshape((2, PIECES, PIECE) + real.shape[1:])
    return np.moveaxis(parts, 0, 1).reshape((PAD,) + real.shape[1:])


def dft_table():
    angle = turns(np.arange(F), np.arange(SAMP), SAMP)
    table = by_pieces(np.cos(angle), -np.sin(angle)) / math.sqrt(SAMP)
    return np.pad(table, ((0, 0), (0, PAD - SAMP))).astype(BF16)


def inverse_table():
    time = (np.arange(SERIES) - HALF) % SAMP
    weight = np.full((F, 1), 2.0)
    weight[0] = weight[-1] = 1.0
    angle = turns(np.arange(F), time, SAMP)
    table = by_pieces(weight * np.cos(angle), -weight * np.sin(angle)).T / math.sqrt(SAMP)
    table = table.reshape(PIECES, SERIES // PIECES, PAD // 128, 128)
    return np.moveaxis(table, 2, 1).reshape(-1, 128).astype(BF16)


def segment_tables():
    angle = turns(np.arange(BINS), np.arange(SPAN), POINTS)
    full = np.stack([np.cos(angle), -np.sin(angle)], axis=1) / math.sqrt(POINTS)
    full = full.reshape(2 * BINS, SPAN)
    full[:, POINTS:] = 0.0
    high = full.astype(BF16)
    low = (full - high.astype(np.float64)).astype(BF16)
    short = np.stack([high[:, :SEG], low[:, :SEG]])
    short = np.stack([short, np.zeros_like(short), short])
    short[2, :, :, SAMP % SEG :] = 0.0
    return high, np.concatenate([short[:, 0], short[:, 1]], axis=2)


def lag_table(windows):
    angle = turns(np.arange(BINS), np.arange(LAGS), POINTS)
    weight = np.full((BINS, 1), 2.0)
    weight[0] = 1.0
    table = np.stack([weight * np.cos(angle), -weight * np.sin(angle)], axis=1)
    return (table / math.sqrt(SAMP * windows)).reshape(2 * BINS, LAGS).astype(BF16)


TALL = 3024
EDGE = 8


def white_kernel(starts, record, table, white, held, raw, wide, samples, spec, power, sems, wins):
    width = record.shape[1]
    rows = 2 * PIECE
    loads = []
    for w in range(2):
        base = jnp.minimum(starts[w] // 16 * 16, record.shape[0] - TALL)
        base = pl.multiple_of(base, 16)
        loads.append(
            pltpu.make_async_copy(record.at[pl.ds(base, TALL)], raw.at[w], wins.at[w])
        )
        loads[w].start()
    pieces = [
        pltpu.make_async_copy(
            table.at[pl.ds(i * rows, rows)], held.at[pl.ds(i * rows, rows)], sems.at[i]
        )
        for i in range(PIECES)
    ]
    for piece in pieces:
        piece.start()
    power[:EDGE, :] = jnp.zeros((EDGE, 2 * width), jnp.float32)
    power[EDGE + PIECES * PIECE :, :] = jnp.zeros((EDGE, 2 * width), jnp.float32)
    for w in range(2):
        shift = starts[w] - jnp.minimum(starts[w] // 16 * 16, record.shape[0] - TALL)
        loads[w].wait()
        wide[w, :TALL, :] = raw[w].astype(jnp.float32)
        wide[w, TALL:, :] = jnp.zeros((wide.shape[1] - TALL, width), jnp.float32)
        samples[:, w * width : (w + 1) * width] = wide[w, pl.ds(shift, PAD), :].astype(jnp.bfloat16)

    def finish(i):
        at = EDGE + i * PIECE
        near = [power[at + d : at + d + PIECE, :] for d in (-1, 0, 1)]
        smooth = (near[0] + near[1] + near[2]) / 3.0
        factor = 1.0 / jnp.maximum(jnp.sqrt(smooth), 0.5)
        for h in range(2):
            part = slice(i * rows + h * PIECE, i * rows + (h + 1) * PIECE)
            white[part, :] = (spec[part, :] * factor).astype(jnp.bfloat16)

    for i in range(PIECES):
        pieces[i].wait()
        part = slice(i * rows, (i + 1) * rows)
        found = jnp.dot(held[part, :], samples[...], preferred_element_type=jnp.float32)
        spec[part, :] = found
        real, imag = found[:PIECE], found[PIECE:]
        power[EDGE + i * PIECE : EDGE + (i + 1) * PIECE, :] = real * real + imag * imag
        if i:
            finish(i - 1)
    finish(PIECES - 1)


def whitened(record, starts):
    width = record.shape[1]
    return pl.pallas_call(
        white_kernel,
        out_shape=jax.ShapeDtypeStruct((PAD, 2 * width), jnp.bfloat16),
        in_specs=[
            pl.BlockSpec(memory_space=pltpu.SMEM),
            pl.BlockSpec(memory_space=pl.ANY),
            pl.BlockSpec(memory_space=pl.ANY),
        ],
        out_specs=pl.BlockSpec(memory_space=pltpu.VMEM),
        scratch_shapes=[
            pltpu.VMEM((PAD, PAD), jnp.bfloat16),
            pltpu.VMEM((2, TALL, width), jnp.bfloat16),
            pltpu.VMEM((2, PAD + 32, width), jnp.float32),
            pltpu.VMEM((PAD, 2 * width), jnp.bfloat16),
            pltpu.VMEM((PAD, 2 * width), jnp.float32),
            pltpu.VMEM((PIECES * PIECE + 2 * EDGE, 2 * width), jnp.float32),
            pltpu.SemaphoreType.DMA((PIECES,)),
            pltpu.SemaphoreType.DMA((2,)),
        ],
        compiler_params=pltpu.CompilerParams(vmem_limit_bytes=62 * 2**20),
        cost_estimate=pl.CostEstimate(
            flops=5 * 10**9, bytes_accessed=22 * 10**6, transcendentals=400_000
        ),
    )(starts, record, jnp.asarray(dft_table()))


FIRST = 8
OUT_ROWS = FIRST + BAND + 9
HELD = 2 * 2 * SLOTS
CHUNK = 16
BOXES = 7
RING = 4
PARTS = 6
BIN_PITCH = 225
NEXT_PITCH = 129
ROW_PITCH = 17
SECOND = 128
EXTRA = 8
EXTRA_ROWS = 384
NO_FAR = 48
KINDS = "XZXXZXZX"
STEPS = (
    "b0", "b1", "s0", "b2", "f", "s1", "s2", "t0", "t1", "b3", "t2",
    "b4", "b5", "s3", "b6", "s5", "b7", "s4", "t3", "l0", "l1", "t5",
    "l2", "s7", "t4", "s6", "l3", "t7", "l4", "l5", "t6", "l7", "l6",
)
MESH = pl.DeviceIdType.MESH


def unrolled(count, step, times):
    def several(i, carry):
        step([i * times + u for u in range(times)])
        return carry

    lax.fori_loop(0, count // times, several, 0)


def pair_kernel(
    white, inverse, fa, fd, lag, out,
    sega, bins, gram, rows, ya, near, pack, extra, far, part, inbox, stage,
    sent, come, sent_y, come_y, local,
):
    width = out.shape[1]
    share = out.shape[0]
    blocks = lax.axis_size("chan")
    i, j = lax.axis_index("tm"), lax.axis_index("chan")
    x, z = lax.rem(i, RING), i // RING
    right = {"tm": z * RING + lax.rem(x + 1, RING)}
    left = {"tm": z * RING + lax.rem(x + RING - 1, RING)}
    other = {"tm": (1 - z) * RING + x}
    odd = lax.rem(j, 2) == 1

    def behind(distance):
        return {"chan": lax.rem(j + blocks + distance, blocks)}

    piece = SERIES // PIECES
    area = piece * (PAD // 128)
    tables = [
        pltpu.make_async_copy(
            inverse.at[pl.ds(c * area, area)], part.at[pl.ds(c % 2 * area, area)], local.at[c % 2]
        )
        for c in range(PIECES)
    ]
    tables[0].start()
    tables[1].start()

    barrier = pltpu.get_barrier_semaphore()
    peers = (right, left, other, behind(-1), behind(1), behind(-2), behind(2))
    for device in peers:
        pl.semaphore_signal(barrier, inc=1, device_id=device, device_id_type=MESH)
    pl.semaphore_wait(barrier, len(peers))

    def remote(source, target, send, receive, device):
        return pltpu.make_async_remote_copy(
            src_ref=source, dst_ref=target, send_sem=send, recv_sem=receive,
            device_id=device, device_id_type=MESH,
        )

    length = SLOTS // PARTS * SEG
    to_near = [
        remote(
            ya.at[pl.ds(SEG + p * length, length)], near.at[pl.ds(p * length, length)],
            sent_y.at[p], come_y.at[p], behind(-1),
        )
        for p in range(PARTS)
    ]
    to_far = [
        remote(pack, far.at[0], sent_y.at[PARTS], come_y.at[PARTS], behind(-2)),
        remote(
            extra, far.at[1, pl.ds(0, EXTRA_ROWS)],
            sent_y.at[PARTS + 1], come_y.at[PARTS + 1], behind(-2),
        ),
    ]
    pass_on = [
        remote(
            near.at[:, pl.ds(w * width, width)], far.at[w],
            sent_y.at[PARTS + 2 + w], come_y.at[PARTS + w], behind(-1),
        )
        for w in range(2)
    ]

    lane = lax.broadcasted_iota(jnp.int32, (SEG, width), 1)
    begun = 0
    for c in range(PIECES):
        tables[c].wait()
        total = jnp.zeros((piece, 2 * width), jnp.float32)
        for p in range(0, PAD // 128, 2):
            first = c % 2 * area + p * piece
            block = jnp.concatenate(
                [part[first : first + piece, :], part[first + piece : first + 2 * piece, :]], 1
            )
            total += jnp.dot(
                block, white[p * 128 : (p + 2) * 128, :], preferred_element_type=jnp.float32
            )
        ya[c * piece : (c + 1) * piece, :] = total.astype(jnp.bfloat16)
        if c + 2 < PIECES:
            tables[c + 2].start()
        while begun < PARTS and SEG + (begun + 1) * length <= (c + 1) * piece:
            to_near[begun].start()
            begun += 1

    def pack_segments(index):
        for s in index:
            block = ya[pl.ds(pl.multiple_of((s + 1) * SEG, SEG), SEG), :].astype(jnp.float32)
            turned = pltpu.roll(block[:, width:], width // 2, 1)
            pack[pl.ds(pl.multiple_of(s * SEG, SEG), SEG), :] = jnp.where(
                lane < width // 2, block[:, :width], turned
            ).astype(jnp.bfloat16)

    def pack_extra(index):
        for e in index:
            total = jnp.zeros((SEG, width), jnp.float32)
            for g in range(PAD // EXTRA_ROWS):
                first = pl.multiple_of((e + 1) * SEG, SEG) + g * EXTRA_ROWS
                block = ya[pl.ds(first, SEG), :].astype(jnp.float32)
                for w in range(2):
                    place = (2 * g + w) * EXTRA
                    turned = pltpu.roll(
                        block[:, w * width : (w + 1) * width], (place + width // 2) % width, 1
                    )
                    total = jnp.where((lane >= place) & (lane < place + EXTRA), turned, total)
            extra[pl.ds(pl.multiple_of(e * SEG, SEG), SEG), :] = total.astype(jnp.bfloat16)

    def far_block(s):
        group, row = s // (EXTRA_ROWS // SEG), lax.rem(s, EXTRA_ROWS // SEG)
        first = far[0, pl.ds(pl.multiple_of(s * SEG, SEG), SEG), :].astype(jnp.float32)
        row = jnp.where(odd, row, s)
        rest = far[1, pl.ds(pl.multiple_of(row * SEG, SEG), SEG), :].astype(jnp.float32)
        half = width // 2
        both = []
        for w in range(2):
            body = first if w == 0 else pltpu.roll(first, half, 1)
            turn = lax.rem(half + width - (2 * group + w) * EXTRA, width)
            both.append(jnp.where(lane < half, body, pltpu.roll(rest, turn, 1)))
        block = jnp.concatenate(
            [jnp.where(odd, both[0], first), jnp.where(odd, both[1], rest)], 1
        )
        return block.astype(jnp.bfloat16)

    def spread(slot, s, spec):
        at = slot * SECOND + s
        bins[pl.ds(at, 2 * BINS, stride=BIN_PITCH), :] = spec[:, :width]
        bins[pl.ds(at + SLOTS, 2 * BINS, stride=BIN_PITCH), :] = spec[:, width:]

    def long_segments(index):
        specs = []
        for s in index:
            block = ya[pl.ds(pl.multiple_of(s * SEG, SEG), SPAN), :]
            specs.append(jnp.dot(fa[...], block, preferred_element_type=jnp.float32))
        for s, spec in zip(index, specs):
            spread(0, s, spec)

    def short_segments(block_of, slot, absent, first, count):
        def step(index):
            specs = []
            for s in index:
                s = first + s
                block = block_of(s)
                twice = jnp.concatenate([block, block], 0)
                kind = jnp.where(s < FULL, 0, jnp.where(s == FULL, 2, 1))
                kind = jnp.where(absent, 1, kind)
                specs.append(jnp.dot(fd[kind], twice, preferred_element_type=jnp.float32))
            for s, spec in zip(index, specs):
                spread(slot, first + s, spec)

        unrolled(count, step, 8)

    def own_block(s):
        return ya[pl.ds(pl.multiple_of((s + 1) * SEG, SEG), SEG), :]

    def near_block(s):
        return near[pl.ds(pl.multiple_of(s * SEG, SEG), SEG), :]

    def of_bin(slot, b):
        first = b * 2 * BIN_PITCH + slot * SECOND
        return bins[pl.ds(first, 2 * SLOTS), :], bins[pl.ds(first + BIN_PITCH, 2 * SLOTS), :]

    def turn_bins(index):
        for b in index:
            sega[b] = jnp.concatenate(of_bin(0, b), 0).astype(jnp.bfloat16).T

    def product(slot, b, first):
        real, imag = [part.astype(jnp.bfloat16) for part in of_bin(slot, b)]
        both = jnp.concatenate(
            [jnp.concatenate([real, imag], 0), jnp.concatenate([-imag, real], 0)], 1
        )
        return jnp.dot(sega[b, first:, :], both, preferred_element_type=jnp.float32)

    def keep(target, pitch, b, cross):
        first = b * 2 * pitch
        target[pl.ds(first, width), :] = cross[:, :width]
        target[pl.ds(first + pitch, width), :] = cross[:, width:]

    def gram_next(index):
        for b, cross in zip(index, [product(1, b, 0) for b in index]):
            keep(gram, NEXT_PITCH, b, cross)

    def gram_own(index):
        for b, cross in zip(index, [product(0, b, 0) for b in index]):
            keep(bins, BIN_PITCH, b, cross)

    tall = width - NO_FAR
    same = lax.broadcasted_iota(jnp.int32, (tall, width), 1)
    same = same > lax.broadcasted_iota(jnp.int32, (tall, width), 0) + NO_FAR

    def gram_far(index):
        crosses = [product(1, b, NO_FAR) for b in index]
        places = [pl.ds((2 * b + h) * BIN_PITCH + NO_FAR, tall) for b in index for h in range(2)]
        before = [bins[place, :] for place in places]
        for e, place in enumerate(places):
            h = e % 2
            cross = crosses[e // 2][:, h * width : (h + 1) * width]
            bins[place, :] = jnp.where(same, before[e], cross)

    def place_next(ahead, c):
        return width + ahead - c

    def place_own(ahead, c):
        return jnp.where(ahead + 7 > c, ahead - c, 2 * width + ahead - c)

    def lag_step(source, pitch, place, base):
        def step(index):
            cross = jnp.concatenate(
                [
                    source[pl.ds(base + c, 2 * BINS, stride=pitch), :].astype(jnp.bfloat16)
                    for c in index
                ],
                1,
            )
            lags = lax.dot_general(
                cross, lag[...], (((0,), (0,)), ((), ())), preferred_element_type=jnp.float32
            )
            for u, c in enumerate(index):
                for e in range(width // 8):
                    k = jnp.clip(place(8 * e, base + c), -FIRST, BAND + 1)
                    at = u * width + 8 * e
                    first = (k + FIRST) * ROW_PITCH + c
                    rows[pl.ds(first, 8, stride=ROW_PITCH), :] = lags[at : at + 8]

        return step

    unrolled(SLOTS, long_segments, 8)
    unrolled(BINS, turn_bins, 8)
    short_segments(own_block, 0, False, 0, SLOTS)
    unrolled(BINS, gram_own, 8)
    unrolled(SLOTS, pack_segments, 8)
    unrolled(EXTRA_ROWS // SEG, pack_extra, 1)
    for p in range(PARTS):
        to_near[p].wait_recv()
        short_segments(near_block, 1, j == blocks - 1, p * (SLOTS // PARTS), SLOTS // PARTS)

    @pl.when(odd)
    def _():
        for copy in to_far + pass_on:
            copy.start()

    unrolled(BINS, gram_next, 8)

    def take_far():
        @pl.when(odd)
        def _():
            for copy in to_far:
                copy.wait_recv()

        @pl.when(jnp.logical_not(odd))
        def _():
            for copy in pass_on:
                copy.wait_recv()

        short_segments(far_block, 1, j >= blocks - 2, 0, SLOTS)
        unrolled(BINS, gram_far, 8)

    def at(column, row):
        return row * RING + lax.rem(column + RING, RING)

    half = share // 2 + 1
    low, high, whole = (0, half), (half, share - half), (0, share)

    def spot(n, place, k, per):
        return pl.multiple_of(((n * per + place) * share + k) * CHUNK, CHUNK)

    def part_at(n, place, k=0, count=1):
        return pl.ds(spot(n, place, k, BAND // share), count * CHUNK)

    def inbox_at(n, place, k=0, count=1):
        return pl.ds(spot(n, place, k, BOXES), count * CHUNK)

    def message(n, m):
        def block(column, row, ks):
            return part.at[part_at(n, at(column, row), *ks)]

        def box(place, ks):
            return inbox.at[inbox_at(n, place, *ks)]

        if KINDS[n] == "X":
            source, target, device = [
                (block(x + 2, 0, whole), box(0, whole), right),
                (block(x + 2, 1, whole), box(1, whole), left),
                (block(x + 1, 1, whole), box(3, whole), right),
                (block(x - 1, 0, whole), box(4, whole), left),
                (block(x + 1, 0, whole), box(2, whole), right),
                (block(x - 1, 1, whole), box(5, whole), left),
                (block(x, 1 - z, whole), box(6, whole), other),
            ][m]
        else:
            four = (0, RING * share)
            source, target, device = [
                (part.at[part_at(n, (1 - z) * RING, *four)], box(0, four), other),
                (block(x + 2, z, low), box(4, low), right),
                (block(x + 2, z, high), box(4, high), left),
                (block(x + 1, z, high), box(5, high), right),
                (block(x - 1, z, low), box(6, low), left),
                (block(x + 1, z, low), box(5, low), right),
                (block(x - 1, z, high), box(6, high), left),
            ][m]
        return remote(source, target, sent.at[n, m], come.at[n, m], device)

    def start(n, *which):
        for m in which:
            message(n, m).start()

    def wait(n, *which):
        for m in which:
            message(n, m).wait_recv()

    def summed(n, place, boxes, k):
        total = part[part_at(n, place, k), :].astype(jnp.float32)
        for box in boxes:
            total += inbox[inbox_at(n, box, k), :].astype(jnp.float32)
        return total

    def plus(n, place, boxes, ks):
        first, count = ks

        def step(index):
            for k in index:
                total = summed(n, place, boxes, first + k)
                part[part_at(n, place, first + k), :] = total.astype(jnp.bfloat16)

        unrolled(count, step, 5 if count % 5 == 0 else count)

    def begin(n):
        unrolled(CHUNK, lag_step(gram, NEXT_PITCH, place_next, n * CHUNK), 8)
        unrolled(CHUNK, lag_step(bins, BIN_PITCH, place_own, n * CHUNK), 8)

        def step(index):
            for k in index:
                for d in range(BAND // share):
                    first = (d * share + k + FIRST + 1) * ROW_PITCH
                    part[part_at(n, d, k), :] = rows[pl.ds(first, CHUNK), :].astype(jnp.bfloat16)

        unrolled(share, step, 5)
        start(n, *((0, 1, 2, 3) if KINDS[n] == "X" else (0,)))

    def second(n):
        if KINDS[n] == "X":
            wait(n, 0, 1)
            plus(n, at(x + 1, 0), [0], whole)
            start(n, 4)
            plus(n, at(x - 1, 1), [1], whole)
            start(n, 5)
        else:
            wait(n, 0)
            for step in (2, 1, 3, 0):
                plus(n, at(x + step, z), [(x + step) % RING], whole)
                start(n, *{2: (1, 2), 1: (3,), 3: (4,), 0: ()}[step])

    def third(n):
        if KINDS[n] == "X":
            wait(n, 2, 3, 4, 5)
            plus(n, at(x, 1 - z), [3 - z, 5 - z], whole)
            start(n, 6)
        else:
            wait(n, 1, 2)
            plus(n, at(x + 1, z), [4], low)
            start(n, 5)
            plus(n, at(x - 1, z), [4], high)
            start(n, 6)

    def last(n):
        if KINDS[n] == "X":
            wait(n, 6)
            boxes = (2 + z, 4 + z, 6)
        else:
            wait(n, 3, 4, 5, 6)
            boxes = (5, 6)

        slot = n % 2
        if n in shown:
            shown[n].wait()

        def step(index):
            for k in index:
                stage[slot, k] = summed(n, at(x, z), boxes, k)

        unrolled(share, step, 5)
        result(n).start()
        for m in range(7):
            message(n, m).wait_send()

    def result(n):
        return pltpu.make_async_copy(
            stage.at[n % 2], out.at[:, pl.ds(n * CHUNK, CHUNK)], local.at[2 + n % 2]
        )

    order = [int(name[1:]) for name in STEPS if name[0] == "l"]
    shown, ending = {}, {}
    for n in order:
        if n % 2 in ending:
            shown[n] = result(ending[n % 2])
        ending[n % 2] = n
    stages = {"b": begin, "s": second, "t": third, "l": last}
    for name in STEPS:
        if name == "f":
            take_far()
        else:
            stages[name[0]](int(name[1:]))

    for n in ending.values():
        result(n).wait()
    for copy in to_near:
        copy.wait_send()

    @pl.when(odd)
    def _():
        for copy in to_far + pass_on:
            copy.wait_send()


def correlate(white, windows, groups):
    width = white.shape[1] // 2
    share = BAND // groups
    chunks = width // CHUNK
    fa, fd = segment_tables()
    vmem = pl.BlockSpec(memory_space=pltpu.VMEM)
    hbm = pl.BlockSpec(memory_space=pl.ANY)
    block = share * CHUNK
    return pl.pallas_call(
        pair_kernel,
        out_shape=jax.ShapeDtypeStruct((share, width, LAGS), jnp.float32),
        in_specs=[vmem, hbm, vmem, vmem, vmem],
        out_specs=hbm,
        scratch_shapes=[
            pltpu.VMEM((BINS, width, HELD), jnp.bfloat16),
            pltpu.VMEM((2 * BINS * BIN_PITCH, width), jnp.float32),
            pltpu.VMEM((2 * BINS * NEXT_PITCH, width), jnp.float32),
            pltpu.VMEM((OUT_ROWS * ROW_PITCH, LAGS), jnp.float32),
            pltpu.VMEM((SERIES, 2 * width), jnp.bfloat16),
            pltpu.VMEM((PAD, 2 * width), jnp.bfloat16),
            pltpu.VMEM((PAD, width), jnp.bfloat16),
            pltpu.VMEM((EXTRA_ROWS, width), jnp.bfloat16),
            pltpu.VMEM((2, PAD, width), jnp.bfloat16),
            pltpu.VMEM((chunks * groups * block, LAGS), jnp.bfloat16),
            pltpu.VMEM((chunks * BOXES * block, LAGS), jnp.bfloat16),
            pltpu.VMEM((2, share, CHUNK, LAGS), jnp.float32),
            pltpu.SemaphoreType.DMA((chunks, 7)),
            pltpu.SemaphoreType.DMA((chunks, 7)),
            pltpu.SemaphoreType.DMA((PARTS + 4,)),
            pltpu.SemaphoreType.DMA((PARTS + 2,)),
            pltpu.SemaphoreType.DMA((4,)),
        ],
        compiler_params=pltpu.CompilerParams(
            vmem_limit_bytes=63 * 2**20, collective_id=0, has_side_effects=True
        ),
        cost_estimate=pl.CostEstimate(flops=6 * 10**9, bytes_accessed=24 * 10**6, transcendentals=0),
    )(
        white,
        jnp.asarray(inverse_table()),
        jnp.asarray(fa),
        jnp.asarray(fd),
        jnp.asarray(lag_table(windows)),
    )


def body(record, starts):
    groups = lax.axis_size("tm")
    white = whitened(record, starts)
    return correlate(white, starts.shape[0] * groups, groups)


def solution(mesh):
    return jax.shard_map(
        body,
        mesh=mesh,
        in_specs=(P("tm", "chan"), P("tm")),
        out_specs=P("tm", "chan", None),
        check_vma=False,
    )
```

```python
import math

import jax
import jax.numpy as jnp
import ml_dtypes
import numpy as np
from jax import lax
from jax.experimental import pallas as pl
from jax.experimental.pallas import tpu as pltpu
from jax.sharding import PartitionSpec as P

SAMP = 3000
F = 1501
PAD = 3072
KEPT = PAD // 2
GROUP = 384
PIECES = 4
BASE = 1664
MID = 1600
BAND = 200
LAGS = 128
HALF = LAGS // 2
SEG = 64
SLOTS = 48
FULL = SAMP // SEG
SPAN = 192
POINTS = 191
BINS = 96
SERIES = SEG * (SLOTS + 2)
BF16 = ml_dtypes.bfloat16


def turns(a, b, period):
    return 2.0 * math.pi * (np.outer(a, b) % period) / period


def bins_of(parity, reverse):
    bins = 2 * np.arange(GROUP) + parity
    bins[bins > F // 2 + 1] = -1
    if reverse:
        bins = np.where(bins >= 0, F - 1 - bins, -1)
        bins[bins <= F // 2] = -1
    else:
        bins[bins > F // 2] = -1
    return bins


def dft_table():
    table = np.zeros((2, 2, GROUP, 2, KEPT), np.float32)
    for parity in range(2):
        bins = np.arange(parity, F // 2 + 2, 2)
        for late in range(2):
            angle = turns(bins, np.arange(late, SAMP, 2), SAMP)
            table[parity, 0, : len(bins), late, : SAMP // 2] = np.cos(angle) / math.sqrt(SAMP)
            table[parity, 1, : len(bins), late, : SAMP // 2] = -np.sin(angle) / math.sqrt(SAMP)
    return table.reshape(KEPT, PAD).astype(BF16)


def inverse_table():
    time = (np.arange(BASE) - HALF) % SAMP
    table = np.zeros((BASE, 2, 2, 2, GROUP), np.float32)
    for parity in range(2):
        for reverse in range(2):
            bins = bins_of(parity, reverse)
            weight = np.where(bins < 0, 0.0, np.where((bins == 0) | (bins == F - 1), 1.0, 2.0))
            weight /= math.sqrt(SAMP)
            angle = turns(time, np.maximum(bins, 0), SAMP)
            table[:, parity, reverse, 0] = weight * np.cos(angle)
            table[:, parity, reverse, 1] = -weight * np.sin(angle)
    table = table.reshape(PIECES, BASE // PIECES, PAD // 128, 128)
    return np.moveaxis(table, 2, 1).reshape(-1, 128).astype(BF16)


def segment_tables():
    angle = turns(np.arange(BINS), np.arange(SPAN), POINTS)
    full = np.stack([np.cos(angle), -np.sin(angle)], axis=1) / math.sqrt(POINTS)
    full = full.reshape(2 * BINS, SPAN)
    full[:, POINTS:] = 0.0
    high = full.astype(BF16)
    low = (full - high.astype(np.float64)).astype(BF16)
    short = np.stack([high[:, :SEG], low[:, :SEG]])
    short = np.stack([short, np.zeros_like(short), short])
    short[2, :, :, SAMP % SEG :] = 0.0
    return high, np.concatenate([short[:, 0], short[:, 1]], axis=2)


def lag_table(windows):
    angle = turns(np.arange(BINS), np.arange(LAGS), POINTS)
    weight = np.full((BINS, 1), 2.0)
    weight[0] = 1.0
    table = np.stack([weight * np.cos(angle), -weight * np.sin(angle)], axis=1)
    return (table / math.sqrt(SAMP * windows)).reshape(2 * BINS, LAGS).astype(BF16)


TALL = 3024
EDGE = 8


def white_kernel(starts, record, table, white, held, raw, wide, samples, spec, power, sems, wins):
    width = record.shape[1]
    loads, shifts = [], []
    for w in range(2):
        base = jnp.minimum(starts[w] // 16 * 16, record.shape[0] - TALL)
        shifts.append(starts[w] - base)
        base = pl.multiple_of(base, 16)
        loads.append(
            pltpu.make_async_copy(record.at[pl.ds(base, TALL)], raw.at[w], wins.at[w])
        )
        loads[w].start()
    pieces = [
        pltpu.make_async_copy(
            table.at[pl.ds(i * GROUP, GROUP)], held.at[pl.ds(i * GROUP, GROUP)], sems.at[i]
        )
        for i in range(PIECES)
    ]
    pieces[0].start()
    pieces[1].start()
    zero = jnp.zeros((EDGE, 2 * width), jnp.float32)
    for parity in range(2):
        for h in range(2):
            power[parity, h, :EDGE, :] = zero
            power[parity, h, EDGE + GROUP :, :] = zero
    for w in range(2):
        loads[w].wait()
        wide[w, :TALL, :] = raw[w].astype(jnp.float32)
        wide[w, TALL:, :] = jnp.zeros((wide.shape[1] - TALL, width), jnp.float32)
        for late in range(2):
            samples[late, :, w * width : (w + 1) * width] = wide[
                w, pl.ds(shifts[w] + late, KEPT, stride=2), :
            ].astype(jnp.bfloat16)

    def group(parity, h, ri):
        first = (parity * 4 + h * 2 + ri) * GROUP
        return slice(first, first + GROUP)

    for parity in range(2):
        squares = []
        for ri in range(2):
            i = parity * 2 + ri
            pieces[i].wait()
            part = slice(i * GROUP, (i + 1) * GROUP)
            early, late = [
                jnp.dot(
                    held[part, e * KEPT : (e + 1) * KEPT], samples[e],
                    preferred_element_type=jnp.float32,
                )
                for e in range(2)
            ]
            if i + 2 < PIECES:
                pieces[i + 2].start()
            both = early + late
            turned = late - early if ri else early - late
            spec[group(parity, 0, ri), :] = both
            spec[group(parity, 1, ri), :] = turned
        for h in range(2):
            real, imag = [spec[group(parity, h, ri), :] for ri in range(2)]
            power[parity, h, EDGE : EDGE + GROUP, :] = real * real + imag * imag

    for parity in range(2):
        for h in range(2):
            for first in range(0, GROUP, 128):
                at = EDGE + first
                beside = (at, at + 1) if parity else (at - 1, at)
                smooth = power[parity, h, at : at + 128, :]
                for place in beside:
                    smooth = smooth + power[1 - parity, h, place : place + 128, :]
                factor = 1.0 / jnp.maximum(jnp.sqrt(smooth / 3.0), 0.5)
                for ri in range(2):
                    start = group(parity, h, ri).start + first
                    part = slice(start, start + 128)
                    white[part, :] = (spec[part, :] * factor).astype(jnp.bfloat16)


def whitened(record, starts):
    width = record.shape[1]
    return pl.pallas_call(
        white_kernel,
        out_shape=jax.ShapeDtypeStruct((PAD, 2 * width), jnp.bfloat16),
        in_specs=[
            pl.BlockSpec(memory_space=pltpu.SMEM),
            pl.BlockSpec(memory_space=pl.ANY),
            pl.BlockSpec(memory_space=pl.ANY),
        ],
        out_specs=pl.BlockSpec(memory_space=pltpu.VMEM),
        scratch_shapes=[
            pltpu.VMEM((KEPT, PAD), jnp.bfloat16),
            pltpu.VMEM((2, TALL, width), jnp.bfloat16),
            pltpu.VMEM((2, PAD + 32, width), jnp.float32),
            pltpu.VMEM((2, KEPT, 2 * width), jnp.bfloat16),
            pltpu.VMEM((PAD, 2 * width), jnp.float32),
            pltpu.VMEM((2, 2, GROUP + 2 * EDGE, 2 * width), jnp.float32),
            pltpu.SemaphoreType.DMA((PIECES,)),
            pltpu.SemaphoreType.DMA((2,)),
        ],
        compiler_params=pltpu.CompilerParams(vmem_limit_bytes=62 * 2**20),
        cost_estimate=pl.CostEstimate(
            flops=5 * 10**9, bytes_accessed=22 * 10**6, transcendentals=400_000
        ),
    )(starts, record, jnp.asarray(dft_table()))


FIRST = 8
OUT_ROWS = FIRST + BAND + 9
HELD = 2 * 2 * SLOTS
CHUNK = 16
BOXES = 7
RING = 4
PARTS = 6
WHEN = ((), (0, 3), (1, 4), (2, 5))
BIN_PITCH = 225
NEXT_PITCH = 129
ROW_PITCH = 17
SECOND = 128
EXTRA = 8
EXTRA_ROWS = 384
NO_FAR = 48
KINDS = "XZXXZZXX"
STEPS = (
    "b0", "b1", "b2", "s0", "f", "s2", "b3", "s1", "t0", "t2", "b4",
    "s3", "b5", "b6", "t1", "b7", "t3", "l0", "l2", "s6", "s4", "l1",
    "s7", "t6", "t4", "s5", "l3", "t7", "l4", "l6", "t5", "l7", "l5",
)
MESH = pl.DeviceIdType.MESH


def unrolled(count, step, times):
    def several(i, carry):
        step([i * times + u for u in range(times)])
        return carry

    lax.fori_loop(0, count // times, several, 0)


def pair_kernel(
    white, inverse, fa, fd, lag, out,
    sega, bins, gram, rows, ya, near, pack, extra, far, part, inbox, stage,
    sent, come, sent_y, come_y, local,
):
    width = out.shape[1]
    share = out.shape[0]
    blocks = lax.axis_size("chan")
    i, j = lax.axis_index("tm"), lax.axis_index("chan")
    x, z = lax.rem(i, RING), i // RING
    right = {"tm": z * RING + lax.rem(x + 1, RING)}
    left = {"tm": z * RING + lax.rem(x + RING - 1, RING)}
    other = {"tm": (1 - z) * RING + x}
    odd = lax.rem(j, 2) == 1

    def behind(distance):
        return {"chan": lax.rem(j + blocks + distance, blocks)}

    piece = BASE // PIECES
    area = piece * (PAD // 128)
    tables = [
        pltpu.make_async_copy(
            inverse.at[pl.ds(c * area, area)], part.at[pl.ds(c % 2 * area, area)], local.at[c % 2]
        )
        for c in range(PIECES)
    ]
    tables[0].start()
    tables[1].start()

    barrier = pltpu.get_barrier_semaphore()
    peers = (right, left, other, behind(-1), behind(1), behind(-2), behind(2))
    for device in peers:
        pl.semaphore_signal(barrier, inc=1, device_id=device, device_id_type=MESH)
    pl.semaphore_wait(barrier, len(peers))

    def remote(source, target, send, receive, device):
        return pltpu.make_async_remote_copy(
            src_ref=source, dst_ref=target, send_sem=send, recv_sem=receive,
            device_id=device, device_id_type=MESH,
        )

    length = SLOTS // PARTS * SEG
    to_near = [
        remote(
            ya.at[pl.ds(SEG + p * length, length)], near.at[pl.ds(p * length, length)],
            sent_y.at[p], come_y.at[p], behind(-1),
        )
        for p in range(PARTS)
    ]
    to_far = [
        remote(pack, far.at[0], sent_y.at[PARTS], come_y.at[PARTS], behind(-2)),
        remote(
            extra, far.at[1, pl.ds(0, EXTRA_ROWS)],
            sent_y.at[PARTS + 1], come_y.at[PARTS + 1], behind(-2),
        ),
    ]
    pass_on = [
        remote(
            near.at[:, pl.ds(w * width, width)], far.at[w],
            sent_y.at[PARTS + 2 + w], come_y.at[PARTS + w], behind(-1),
        )
        for w in range(2)
    ]

    lane = lax.broadcasted_iota(jnp.int32, (SEG, width), 1)
    done = MID
    for c in range(PIECES):
        tables[c].wait()
        halves = []
        for parity in range(2):
            total = jnp.zeros((piece, 2 * width), jnp.float32)
            for p in range(parity * KEPT // 128, (parity + 1) * KEPT // 128, 2):
                first = c % 2 * area + p * piece
                block = jnp.concatenate(
                    [part[first : first + piece, :], part[first + piece : first + 2 * piece, :]], 1
                )
                total += jnp.dot(
                    block, white[p * 128 : (p + 2) * 128, :], preferred_element_type=jnp.float32
                )
            halves.append(total)
        if c + 2 < PIECES:
            tables[c + 2].start()
        first, end = c * piece, (c + 1) * piece
        kept = min(end, MID) - first
        ya[first : first + kept, :] = (halves[0] + halves[1])[:kept].astype(jnp.bfloat16)
        later = halves[0] - halves[1]
        for w in range(2):
            rows[w * BASE + first : w * BASE + end, :] = later[:, w * width : (w + 1) * width]
        ready = (end + SAMP // 2) // 16 * 16
        for w in range(2):
            source = slice(w * BASE + done - SAMP // 2, w * BASE + ready - SAMP // 2)
            ya[done:ready, w * width : (w + 1) * width] = rows[source, :].astype(jnp.bfloat16)
        done = ready
        for p in WHEN[c]:
            to_near[p].start()
    ya[done:, :] = jnp.zeros((SERIES - done, 2 * width), jnp.bfloat16)

    def pack_segments(index):
        for s in index:
            block = ya[pl.ds(pl.multiple_of((s + 1) * SEG, SEG), SEG), :].astype(jnp.float32)
            turned = pltpu.roll(block[:, width:], width // 2, 1)
            pack[pl.ds(pl.multiple_of(s * SEG, SEG), SEG), :] = jnp.where(
                lane < width // 2, block[:, :width], turned
            ).astype(jnp.bfloat16)

    def pack_extra(index):
        for e in index:
            total = jnp.zeros((SEG, width), jnp.float32)
            for g in range(PAD // EXTRA_ROWS):
                first = pl.multiple_of((e + 1) * SEG, SEG) + g * EXTRA_ROWS
                block = ya[pl.ds(first, SEG), :].astype(jnp.float32)
                for w in range(2):
                    place = (2 * g + w) * EXTRA
                    turned = pltpu.roll(
                        block[:, w * width : (w + 1) * width], (place + width // 2) % width, 1
                    )
                    total = jnp.where((lane >= place) & (lane < place + EXTRA), turned, total)
            extra[pl.ds(pl.multiple_of(e * SEG, SEG), SEG), :] = total.astype(jnp.bfloat16)

    def far_block(s):
        group, row = s // (EXTRA_ROWS // SEG), lax.rem(s, EXTRA_ROWS // SEG)
        first = far[0, pl.ds(pl.multiple_of(s * SEG, SEG), SEG), :].astype(jnp.float32)
        row = jnp.where(odd, row, s)
        rest = far[1, pl.ds(pl.multiple_of(row * SEG, SEG), SEG), :].astype(jnp.float32)
        half = width // 2
        both = []
        for w in range(2):
            body = first if w == 0 else pltpu.roll(first, half, 1)
            turn = lax.rem(half + width - (2 * group + w) * EXTRA, width)
            both.append(jnp.where(lane < half, body, pltpu.roll(rest, turn, 1)))
        block = jnp.concatenate(
            [jnp.where(odd, both[0], first), jnp.where(odd, both[1], rest)], 1
        )
        return block.astype(jnp.bfloat16)

    def spread(slot, s, spec):
        at = slot * SECOND + s
        bins[pl.ds(at, 2 * BINS, stride=BIN_PITCH), :] = spec[:, :width]
        bins[pl.ds(at + SLOTS, 2 * BINS, stride=BIN_PITCH), :] = spec[:, width:]

    def long_segments(index):
        specs = []
        for s in index:
            block = ya[pl.ds(pl.multiple_of(s * SEG, SEG), SPAN), :]
            specs.append(jnp.dot(fa[...], block, preferred_element_type=jnp.float32))
        for s, spec in zip(index, specs):
            spread(0, s, spec)

    def short_segments(block_of, slot, absent, first, count):
        def step(index):
            specs = []
            for s in index:
                s = first + s
                block = block_of(s)
                twice = jnp.concatenate([block, block], 0)
                kind = jnp.where(s < FULL, 0, jnp.where(s == FULL, 2, 1))
                kind = jnp.where(absent, 1, kind)
                specs.append(jnp.dot(fd[kind], twice, preferred_element_type=jnp.float32))
            for s, spec in zip(index, specs):
                spread(slot, first + s, spec)

        unrolled(count, step, 8)

    def own_block(s):
        return ya[pl.ds(pl.multiple_of((s + 1) * SEG, SEG), SEG), :]

    def near_block(s):
        return near[pl.ds(pl.multiple_of(s * SEG, SEG), SEG), :]

    def of_bin(slot, b):
        first = b * 2 * BIN_PITCH + slot * SECOND
        return bins[pl.ds(first, 2 * SLOTS), :], bins[pl.ds(first + BIN_PITCH, 2 * SLOTS), :]

    def turn_bins(index):
        for b in index:
            sega[b] = jnp.concatenate(of_bin(0, b), 0).astype(jnp.bfloat16).T

    def product(slot, b, first):
        real, imag = [part.astype(jnp.bfloat16) for part in of_bin(slot, b)]
        both = jnp.concatenate(
            [jnp.concatenate([real, imag], 0), jnp.concatenate([-imag, real], 0)], 1
        )
        return jnp.dot(sega[b, first:, :], both, preferred_element_type=jnp.float32)

    def keep(target, pitch, b, cross):
        first = b * 2 * pitch
        target[pl.ds(first, width), :] = cross[:, :width]
        target[pl.ds(first + pitch, width), :] = cross[:, width:]

    def gram_next(index):
        for b, cross in zip(index, [product(1, b, 0) for b in index]):
            keep(gram, NEXT_PITCH, b, cross)

    def gram_own(index):
        for b, cross in zip(index, [product(0, b, 0) for b in index]):
            keep(bins, BIN_PITCH, b, cross)

    tall = width - NO_FAR
    same = lax.broadcasted_iota(jnp.int32, (tall, width), 1)
    same = same > lax.broadcasted_iota(jnp.int32, (tall, width), 0) + NO_FAR

    def gram_far(index):
        crosses = [product(1, b, NO_FAR) for b in index]
        places = [pl.ds((2 * b + h) * BIN_PITCH + NO_FAR, tall) for b in index for h in range(2)]
        before = [bins[place, :] for place in places]
        for e, place in enumerate(places):
            h = e % 2
            cross = crosses[e // 2][:, h * width : (h + 1) * width]
            bins[place, :] = jnp.where(same, before[e], cross)

    def place_next(ahead, c):
        return width + ahead - c

    def place_own(ahead, c):
        return jnp.where(ahead + 7 > c, ahead - c, 2 * width + ahead - c)

    def lag_step(source, pitch, place, base):
        def step(index):
            cross = jnp.concatenate(
                [
                    source[pl.ds(base + c, 2 * BINS, stride=pitch), :].astype(jnp.bfloat16)
                    for c in index
                ],
                1,
            )
            lags = lax.dot_general(
                cross, lag[...], (((0,), (0,)), ((), ())), preferred_element_type=jnp.float32
            )
            for u, c in enumerate(index):
                for e in range(width // 8):
                    k = jnp.clip(place(8 * e, base + c), -FIRST, BAND + 1)
                    at = u * width + 8 * e
                    first = (k + FIRST) * ROW_PITCH + c
                    rows[pl.ds(first, 8, stride=ROW_PITCH), :] = lags[at : at + 8]

        return step

    unrolled(SLOTS, long_segments, 8)
    unrolled(BINS, turn_bins, 8)
    short_segments(own_block, 0, False, 0, SLOTS)
    unrolled(BINS, gram_own, 8)
    unrolled(SLOTS, pack_segments, 8)
    unrolled(EXTRA_ROWS // SEG, pack_extra, 1)
    for p in sum(WHEN, ()):
        to_near[p].wait_recv()
        if p == WHEN[-1][0]:

            @pl.when(odd)
            def _():
                for copy in to_far:
                    copy.start()

        short_segments(near_block, 1, j == blocks - 1, p * (SLOTS // PARTS), SLOTS // PARTS)

    @pl.when(odd)
    def _():
        for copy in pass_on:
            copy.start()

    unrolled(BINS, gram_next, 8)

    def take_far():
        @pl.when(odd)
        def _():
            for copy in to_far:
                copy.wait_recv()

        @pl.when(jnp.logical_not(odd))
        def _():
            for copy in pass_on:
                copy.wait_recv()

        short_segments(far_block, 1, j >= blocks - 2, 0, SLOTS)
        unrolled(BINS, gram_far, 8)

    def at(column, row):
        return row * RING + lax.rem(column + RING, RING)

    half = share // 2 + 1
    low, high, whole = (0, half), (half, share - half), (0, share)

    def spot(n, place, k, per):
        return pl.multiple_of(((n * per + place) * share + k) * CHUNK, CHUNK)

    def part_at(n, place, k=0, count=1):
        return pl.ds(spot(n, place, k, BAND // share), count * CHUNK)

    def inbox_at(n, place, k=0, count=1):
        return pl.ds(spot(n, place, k, BOXES), count * CHUNK)

    def message(n, m):
        def block(column, row, ks):
            return part.at[part_at(n, at(column, row), *ks)]

        def box(place, ks):
            return inbox.at[inbox_at(n, place, *ks)]

        if KINDS[n] == "X":
            source, target, device = [
                (block(x + 2, 0, whole), box(0, whole), right),
                (block(x + 2, 1, whole), box(1, whole), left),
                (block(x + 1, 1, whole), box(3, whole), right),
                (block(x - 1, 0, whole), box(4, whole), left),
                (block(x + 1, 0, whole), box(2, whole), right),
                (block(x - 1, 1, whole), box(5, whole), left),
                (block(x, 1 - z, whole), box(6, whole), other),
            ][m]
        else:
            four = (0, RING * share)
            source, target, device = [
                (part.at[part_at(n, (1 - z) * RING, *four)], box(0, four), other),
                (block(x + 2, z, low), box(4, low), right),
                (block(x + 2, z, high), box(4, high), left),
                (block(x + 1, z, high), box(5, high), right),
                (block(x - 1, z, low), box(6, low), left),
                (block(x + 1, z, low), box(5, low), right),
                (block(x - 1, z, high), box(6, high), left),
            ][m]
        return remote(source, target, sent.at[n, m], come.at[n, m], device)

    def start(n, *which):
        for m in which:
            message(n, m).start()

    def wait(n, *which):
        for m in which:
            message(n, m).wait_recv()

    def summed(n, place, boxes, k):
        total = part[part_at(n, place, k), :].astype(jnp.float32)
        for box in boxes:
            total += inbox[inbox_at(n, box, k), :].astype(jnp.float32)
        return total

    def plus(n, place, boxes, ks):
        first, count = ks

        def step(index):
            for k in index:
                total = summed(n, place, boxes, first + k)
                part[part_at(n, place, first + k), :] = total.astype(jnp.bfloat16)

        unrolled(count, step, 5 if count % 5 == 0 else count)

    def begin(n):
        unrolled(CHUNK, lag_step(gram, NEXT_PITCH, place_next, n * CHUNK), 8)
        unrolled(CHUNK, lag_step(bins, BIN_PITCH, place_own, n * CHUNK), 8)

        def step(index):
            for k in index:
                for d in range(BAND // share):
                    first = (d * share + k + FIRST + 1) * ROW_PITCH
                    part[part_at(n, d, k), :] = rows[pl.ds(first, CHUNK), :].astype(jnp.bfloat16)

        unrolled(share, step, 5)
        start(n, *((0, 1, 2, 3) if KINDS[n] == "X" else (0,)))

    def second(n):
        if KINDS[n] == "X":
            wait(n, 0, 1)
            plus(n, at(x + 1, 0), [0], whole)
            start(n, 4)
            plus(n, at(x - 1, 1), [1], whole)
            start(n, 5)
        else:
            wait(n, 0)
            for step in (2, 1, 3, 0):
                plus(n, at(x + step, z), [(x + step) % RING], whole)
                start(n, *{2: (1, 2), 1: (3,), 3: (4,), 0: ()}[step])

    def third(n):
        if KINDS[n] == "X":
            wait(n, 2, 3, 4, 5)
            plus(n, at(x, 1 - z), [3 - z, 5 - z], whole)
            start(n, 6)
        else:
            wait(n, 1, 2)
            plus(n, at(x + 1, z), [4], low)
            start(n, 5)
            plus(n, at(x - 1, z), [4], high)
            start(n, 6)

    def last(n):
        if KINDS[n] == "X":
            wait(n, 6)
            boxes = (2 + z, 4 + z, 6)
        else:
            wait(n, 3, 4, 5, 6)
            boxes = (5, 6)

        slot = n % 2
        if n in shown:
            shown[n].wait()

        def step(index):
            for k in index:
                stage[slot, k] = summed(n, at(x, z), boxes, k)

        unrolled(share, step, 5)
        result(n).start()
        for m in range(7):
            message(n, m).wait_send()

    def result(n):
        return pltpu.make_async_copy(
            stage.at[n % 2], out.at[:, pl.ds(n * CHUNK, CHUNK)], local.at[2 + n % 2]
        )

    order = [int(name[1:]) for name in STEPS if name[0] == "l"]
    shown, ending = {}, {}
    for n in order:
        if n % 2 in ending:
            shown[n] = result(ending[n % 2])
        ending[n % 2] = n
    stages = {"b": begin, "s": second, "t": third, "l": last}
    for name in STEPS:
        if name == "f":
            take_far()
        else:
            stages[name[0]](int(name[1:]))

    for n in ending.values():
        result(n).wait()
    for copy in to_near:
        copy.wait_send()

    @pl.when(odd)
    def _():
        for copy in to_far + pass_on:
            copy.wait_send()


def correlate(white, windows, groups):
    width = white.shape[1] // 2
    share = BAND // groups
    chunks = width // CHUNK
    fa, fd = segment_tables()
    vmem = pl.BlockSpec(memory_space=pltpu.VMEM)
    hbm = pl.BlockSpec(memory_space=pl.ANY)
    block = share * CHUNK
    return pl.pallas_call(
        pair_kernel,
        out_shape=jax.ShapeDtypeStruct((share, width, LAGS), jnp.float32),
        in_specs=[vmem, hbm, vmem, vmem, vmem],
        out_specs=hbm,
        scratch_shapes=[
            pltpu.VMEM((BINS, width, HELD), jnp.bfloat16),
            pltpu.VMEM((2 * BINS * BIN_PITCH, width), jnp.float32),
            pltpu.VMEM((2 * BINS * NEXT_PITCH, width), jnp.float32),
            pltpu.VMEM((OUT_ROWS * ROW_PITCH, LAGS), jnp.float32),
            pltpu.VMEM((SERIES, 2 * width), jnp.bfloat16),
            pltpu.VMEM((PAD, 2 * width), jnp.bfloat16),
            pltpu.VMEM((PAD, width), jnp.bfloat16),
            pltpu.VMEM((EXTRA_ROWS, width), jnp.bfloat16),
            pltpu.VMEM((2, PAD, width), jnp.bfloat16),
            pltpu.VMEM((chunks * groups * block, LAGS), jnp.bfloat16),
            pltpu.VMEM((chunks * BOXES * block, LAGS), jnp.bfloat16),
            pltpu.VMEM((2, share, CHUNK, LAGS), jnp.float32),
            pltpu.SemaphoreType.DMA((chunks, 7)),
            pltpu.SemaphoreType.DMA((chunks, 7)),
            pltpu.SemaphoreType.DMA((PARTS + 4,)),
            pltpu.SemaphoreType.DMA((PARTS + 2,)),
            pltpu.SemaphoreType.DMA((4,)),
        ],
        compiler_params=pltpu.CompilerParams(
            vmem_limit_bytes=63 * 2**20, collective_id=0, has_side_effects=True
        ),
        cost_estimate=pl.CostEstimate(flops=6 * 10**9, bytes_accessed=24 * 10**6, transcendentals=0),
    )(
        white,
        jnp.asarray(inverse_table()),
        jnp.asarray(fa),
        jnp.asarray(fd),
        jnp.asarray(lag_table(windows)),
    )


def body(record, starts):
    groups = lax.axis_size("tm")
    white = whitened(record, starts)
    return correlate(white, starts.shape[0] * groups, groups)


def solution(mesh):
    return jax.shard_map(
        body,
        mesh=mesh,
        in_specs=(P("tm", "chan"), P("tm")),
        out_specs=P("tm", "chan", None),
        check_vma=False,
    )
```

```python
import functools
import math

import jax
import jax.numpy as jnp
import ml_dtypes
import numpy as np
from jax import lax
from jax.experimental import pallas as pl
from jax.experimental.pallas import tpu as pltpu
from jax.sharding import PartitionSpec as P

SAMP = 3000
F = 1501
PAD = 3072
KEPT = PAD // 2
GROUP = 384
PIECES = 4
BASE = 1664
MID = 1600
BAND = 200
LAGS = 128
HALF = LAGS // 2
SEG = 64
SLOTS = 48
FULL = SAMP // SEG
SPAN = 192
POINTS = 191
BINS = 96
SERIES = SEG * (SLOTS + 2)
BF16 = ml_dtypes.bfloat16


def turns(a, b, period):
    return 2.0 * math.pi * (np.outer(a, b) % period) / period


def bins_of(parity, reverse):
    bins = 2 * np.arange(GROUP) + parity
    bins[bins > F // 2 + 1] = -1
    if reverse:
        bins = np.where(bins >= 0, F - 1 - bins, -1)
        bins[bins <= F // 2] = -1
    else:
        bins[bins > F // 2] = -1
    return bins


def dft_table():
    table = np.zeros((2, 2, GROUP, 2, KEPT), np.float32)
    for parity in range(2):
        bins = np.arange(parity, F // 2 + 2, 2)
        for late in range(2):
            angle = turns(bins, np.arange(late, SAMP, 2), SAMP)
            table[parity, 0, : len(bins), late, : SAMP // 2] = np.cos(angle) / math.sqrt(SAMP)
            table[parity, 1, : len(bins), late, : SAMP // 2] = -np.sin(angle) / math.sqrt(SAMP)
    return table.reshape(KEPT, PAD).astype(BF16)


def inverse_table():
    time = (np.arange(BASE) - HALF) % SAMP
    table = np.zeros((BASE, 2, 2, 2, GROUP), np.float32)
    for parity in range(2):
        for reverse in range(2):
            bins = bins_of(parity, reverse)
            weight = np.where(bins < 0, 0.0, np.where((bins == 0) | (bins == F - 1), 1.0, 2.0))
            weight /= math.sqrt(SAMP)
            angle = turns(time, np.maximum(bins, 0), SAMP)
            table[:, parity, reverse, 0] = weight * np.cos(angle)
            table[:, parity, reverse, 1] = -weight * np.sin(angle)
    table = table.reshape(PIECES, BASE // PIECES, PAD // 128, 128)
    return np.moveaxis(table, 2, 1).reshape(-1, 128).astype(BF16)


def segment_tables():
    angle = turns(np.arange(BINS), np.arange(SPAN), POINTS)
    full = np.stack([np.cos(angle), -np.sin(angle)], axis=1) / math.sqrt(POINTS)
    full = full.reshape(2 * BINS, SPAN)
    full[:, POINTS:] = 0.0
    high = full.astype(BF16)
    low = (full - high.astype(np.float64)).astype(BF16)
    short = np.stack([high[:, :SEG], low[:, :SEG]])
    short = np.stack([short, np.zeros_like(short), short])
    short[2, :, :, SAMP % SEG :] = 0.0
    return high, np.concatenate([short[:, 0], short[:, 1]], axis=2)


def lag_table(windows):
    angle = turns(np.arange(BINS), np.arange(LAGS), POINTS)
    weight = np.full((BINS, 1), 2.0)
    weight[0] = 1.0
    table = np.stack([weight * np.cos(angle), -weight * np.sin(angle)], axis=1)
    return (table / math.sqrt(SAMP * windows)).reshape(2 * BINS, LAGS).astype(BF16)


TALL = 3024
EDGE = 8


def white_kernel(starts, record, table, white, held, raw, wide, samples, spec, power, sems, wins):
    width = record.shape[1]
    loads, shifts = [], []
    for w in range(2):
        base = jnp.minimum(starts[w] // 16 * 16, record.shape[0] - TALL)
        shifts.append(starts[w] - base)
        base = pl.multiple_of(base, 16)
        loads.append(
            pltpu.make_async_copy(record.at[pl.ds(base, TALL)], raw.at[w], wins.at[w])
        )
        loads[w].start()
    pieces = [
        pltpu.make_async_copy(
            table.at[pl.ds(i * 2 * GROUP, 2 * GROUP)], held.at[pl.ds(i * 2 * GROUP, 2 * GROUP)],
            sems.at[i],
        )
        for i in range(2)
    ]
    pieces[0].start()
    zero = jnp.zeros((EDGE, 2 * width), jnp.float32)
    for parity in range(2):
        for h in range(2):
            power[parity, h, :EDGE, :] = zero
            power[parity, h, EDGE + GROUP :, :] = zero
    for w in range(2):
        loads[w].wait()
        wide[w, :TALL, :] = raw[w].astype(jnp.float32)
        wide[w, TALL:, :] = jnp.zeros((wide.shape[1] - TALL, width), jnp.float32)
        for late in range(2):
            samples[late, :, w * width : (w + 1) * width] = wide[
                w, pl.ds(shifts[w] + late, KEPT, stride=2), :
            ].astype(jnp.bfloat16)

    def group(parity, h, ri):
        first = (parity * 4 + h * 2 + ri) * GROUP
        return slice(first, first + GROUP)

    for parity in range(2):
        pieces[parity].wait()
        if parity == 0:
            pieces[1].start()
        part = slice(parity * 2 * GROUP, (parity + 1) * 2 * GROUP)
        early, late = [
            jnp.dot(
                held[part, e * KEPT : (e + 1) * KEPT], samples[e],
                preferred_element_type=jnp.float32,
            )
            for e in range(2)
        ]
        for ri in range(2):
            one, two = [found[ri * GROUP : (ri + 1) * GROUP] for found in (early, late)]
            spec[group(parity, 0, ri), :] = one + two
            spec[group(parity, 1, ri), :] = two - one if ri else one - two
        for h in range(2):
            real, imag = [spec[group(parity, h, ri), :] for ri in range(2)]
            power[parity, h, EDGE : EDGE + GROUP, :] = real * real + imag * imag

    for parity in range(2):
        for h in range(2):
            for first in range(0, GROUP, 128):
                at = EDGE + first
                beside = (at, at + 1) if parity else (at - 1, at)
                smooth = power[parity, h, at : at + 128, :]
                for place in beside:
                    smooth = smooth + power[1 - parity, h, place : place + 128, :]
                factor = 1.0 / jnp.maximum(jnp.sqrt(smooth / 3.0), 0.5)
                for ri in range(2):
                    start = group(parity, h, ri).start + first
                    part = slice(start, start + 128)
                    white[part, :] = (spec[part, :] * factor).astype(jnp.bfloat16)


def whitened(record, starts):
    width = record.shape[1]
    return pl.pallas_call(
        white_kernel,
        out_shape=jax.ShapeDtypeStruct((PAD, 2 * width), jnp.bfloat16),
        in_specs=[
            pl.BlockSpec(memory_space=pltpu.SMEM),
            pl.BlockSpec(memory_space=pl.ANY),
            pl.BlockSpec(memory_space=pl.ANY),
        ],
        out_specs=pl.BlockSpec(memory_space=pltpu.VMEM),
        scratch_shapes=[
            pltpu.VMEM((KEPT, PAD), jnp.bfloat16),
            pltpu.VMEM((2, TALL, width), jnp.bfloat16),
            pltpu.VMEM((2, PAD + 32, width), jnp.float32),
            pltpu.VMEM((2, KEPT, 2 * width), jnp.bfloat16),
            pltpu.VMEM((PAD, 2 * width), jnp.float32),
            pltpu.VMEM((2, 2, GROUP + 2 * EDGE, 2 * width), jnp.float32),
            pltpu.SemaphoreType.DMA((PIECES,)),
            pltpu.SemaphoreType.DMA((2,)),
        ],
        compiler_params=pltpu.CompilerParams(vmem_limit_bytes=62 * 2**20),
        cost_estimate=pl.CostEstimate(
            flops=5 * 10**9, bytes_accessed=22 * 10**6, transcendentals=400_000
        ),
    )(starts, record, jnp.asarray(dft_table()))


FIRST = 8
OUT_ROWS = FIRST + BAND + 9
HELD = 2 * 2 * SLOTS
CHUNK = 16
BOXES = 7
RING = 4
BIN_PITCH = 225
NEXT_PITCH = 129
ROW_PITCH = 17
SECOND = 128
EXTRA = 8
EXTRA_ROWS = 384
NO_FAR = 48
KINDS = "XZXXZZXX"
STEPS = (
    "b0", "b1", "b2", "s0", "f", "s2", "b3", "s1", "t0", "t2", "b4",
    "s3", "b5", "b6", "t1", "b7", "t3", "l0", "l2", "s6", "s4", "l1",
    "s7", "t6", "t4", "s5", "l3", "t7", "l4", "l6", "t5", "l7", "l5",
)
MESH = pl.DeviceIdType.MESH


def unrolled(count, step, times):
    def several(i, carry):
        step([i * times + u for u in range(times)])
        return carry

    lax.fori_loop(0, count // times, several, 0)


def pair_kernel(
    white, inverse, fa, fd, lag, out,
    sega, bins, gram, rows, ya, near, pack, extra, far, part, inbox, stage,
    sent, come, sent_y, come_y, local,
):
    width = out.shape[1]
    share = out.shape[0]
    blocks = lax.axis_size("chan")
    i, j = lax.axis_index("tm"), lax.axis_index("chan")
    x, z = lax.rem(i, RING), i // RING
    right = {"tm": z * RING + lax.rem(x + 1, RING)}
    left = {"tm": z * RING + lax.rem(x + RING - 1, RING)}
    other = {"tm": (1 - z) * RING + x}
    odd = lax.rem(j, 2) == 1

    def behind(distance):
        return {"chan": lax.rem(j + blocks + distance, blocks)}

    piece = BASE // PIECES
    area = piece * (PAD // 128)
    tables = [
        pltpu.make_async_copy(
            inverse.at[pl.ds(c * area, area)], part.at[pl.ds(c % 2 * area, area)], local.at[c % 2]
        )
        for c in range(PIECES)
    ]
    tables[0].start()
    tables[1].start()

    barrier = pltpu.get_barrier_semaphore()
    peers = (right, left, other, behind(-1), behind(1), behind(-2), behind(2))
    for device in peers:
        pl.semaphore_signal(barrier, inc=1, device_id=device, device_id_type=MESH)
    pl.semaphore_wait(barrier, len(peers))

    def remote(source, target, send, receive, device):
        return pltpu.make_async_remote_copy(
            src_ref=source, dst_ref=target, send_sem=send, recv_sem=receive,
            device_id=device, device_id_type=MESH,
        )

    spans, turns_long, turns_short = [], [], []
    done, began, fresh = MID, (0, MID // SEG), (0, MID // SEG - 1)
    for c in range(PIECES):
        first, end = c * piece, (c + 1) * piece
        ready = (end + SAMP // 2) // 16 * 16
        low_end = min(end, MID)
        spans.append(((max(first, SEG), low_end), (done, min(ready, SEG * (SLOTS + 1)))))
        done = ready
        final = c == PIECES - 1
        stop = (
            MID // SEG if final else (end - SPAN) // SEG + 1,
            SLOTS if final else (ready - SPAN) // SEG + 1,
        )
        turns_long.append([s for h in range(2) for s in range(began[h], stop[h])])
        began = stop
        stop = (
            MID // SEG - 1 if final else end // SEG - 1,
            SLOTS if final else ready // SEG - 1,
        )
        turns_short.append([s for h in range(2) for s in range(fresh[h], stop[h])])
        fresh = stop
    parts = 2 * PIECES
    to_near = [
        remote(
            ya.at[pl.ds(first, end - first)], near.at[pl.ds(first - SEG, end - first)],
            sent_y.at[2 * c + h], come_y.at[2 * c + h], behind(-1),
        )
        for c in range(PIECES)
        for h, (first, end) in enumerate(spans[c])
    ]
    to_far = [
        remote(pack, far.at[0], sent_y.at[parts], come_y.at[parts], behind(-2)),
        remote(
            extra, far.at[1, pl.ds(0, EXTRA_ROWS)],
            sent_y.at[parts + 1], come_y.at[parts + 1], behind(-2),
        ),
    ]
    pass_on = [
        remote(
            near.at[:, pl.ds(w * width, width)], far.at[w],
            sent_y.at[parts + 2 + w], come_y.at[parts + w], behind(-1),
        )
        for w in range(2)
    ]

    lane = lax.broadcasted_iota(jnp.int32, (SEG, width), 1)
    def pack_segments(index):
        for s in index:
            block = ya[pl.ds(pl.multiple_of((s + 1) * SEG, SEG), SEG), :].astype(jnp.float32)
            turned = pltpu.roll(block[:, width:], width // 2, 1)
            pack[pl.ds(pl.multiple_of(s * SEG, SEG), SEG), :] = jnp.where(
                lane < width // 2, block[:, :width], turned
            ).astype(jnp.bfloat16)

    def pack_extra(index):
        for e in index:
            total = jnp.zeros((SEG, width), jnp.float32)
            for g in range(PAD // EXTRA_ROWS):
                first = pl.multiple_of((e + 1) * SEG, SEG) + g * EXTRA_ROWS
                block = ya[pl.ds(first, SEG), :].astype(jnp.float32)
                for w in range(2):
                    place = (2 * g + w) * EXTRA
                    turned = pltpu.roll(
                        block[:, w * width : (w + 1) * width], (place + width // 2) % width, 1
                    )
                    total = jnp.where((lane >= place) & (lane < place + EXTRA), turned, total)
            extra[pl.ds(pl.multiple_of(e * SEG, SEG), SEG), :] = total.astype(jnp.bfloat16)

    def far_block(s):
        group, row = s // (EXTRA_ROWS // SEG), lax.rem(s, EXTRA_ROWS // SEG)
        first = far[0, pl.ds(pl.multiple_of(s * SEG, SEG), SEG), :].astype(jnp.float32)
        row = jnp.where(odd, row, s)
        rest = far[1, pl.ds(pl.multiple_of(row * SEG, SEG), SEG), :].astype(jnp.float32)
        half = width // 2
        both = []
        for w in range(2):
            body = first if w == 0 else pltpu.roll(first, half, 1)
            turn = lax.rem(half + width - (2 * group + w) * EXTRA, width)
            both.append(jnp.where(lane < half, body, pltpu.roll(rest, turn, 1)))
        block = jnp.concatenate(
            [jnp.where(odd, both[0], first), jnp.where(odd, both[1], rest)], 1
        )
        return block.astype(jnp.bfloat16)

    def spread(slot, s, spec):
        at = slot * SECOND + s
        bins[pl.ds(at, 2 * BINS, stride=BIN_PITCH), :] = spec[:, :width]
        bins[pl.ds(at + SLOTS, 2 * BINS, stride=BIN_PITCH), :] = spec[:, width:]

    def long_segments(index):
        specs = []
        for s in index:
            block = ya[s * SEG : s * SEG + SPAN, :]
            specs.append(jnp.dot(fa[...], block, preferred_element_type=jnp.float32))
        for s, spec in zip(index, specs):
            spread(1, s, spec)

    def short_batch(block_of, slot, absent, index):
        specs = []
        for s in index:
            block = block_of(s)
            twice = jnp.concatenate([block, block], 0)
            if isinstance(s, int):
                kind = 0 if s < FULL else 2 if s == FULL else 1
            else:
                kind = jnp.where(s < FULL, 0, jnp.where(s == FULL, 2, 1))
            if absent is not None:
                kind = jnp.where(absent, 1, kind)
            specs.append(jnp.dot(fd[kind], twice, preferred_element_type=jnp.float32))
        for s, spec in zip(index, specs):
            spread(slot, s, spec)

    def short_segments(block_of, slot, absent):
        unrolled(SLOTS, functools.partial(short_batch, block_of, slot, absent), 8)

    def place_of(s):
        return s * SEG if isinstance(s, int) else pl.multiple_of(s * SEG, SEG)

    def own_block(s):
        return ya[pl.ds(place_of(s + 1), SEG), :]

    def near_block(s):
        return near[pl.ds(place_of(s), SEG), :]

    def of_bin(slot, b):
        first = b * 2 * BIN_PITCH + slot * SECOND
        return bins[pl.ds(first, 2 * SLOTS), :], bins[pl.ds(first + BIN_PITCH, 2 * SLOTS), :]

    def product(slot, b, first):
        real, imag = [part.astype(jnp.bfloat16) for part in of_bin(slot, b)]
        both = jnp.concatenate(
            [jnp.concatenate([real, imag], 0), jnp.concatenate([-imag, real], 0)], 1
        )
        return jnp.dot(sega[b, first:, :], both, preferred_element_type=jnp.float32)

    def keep(target, pitch, b, cross):
        first = b * 2 * pitch
        target[pl.ds(first, width), :] = cross[:, :width]
        target[pl.ds(first + pitch, width), :] = cross[:, width:]

    def gram_next(index):
        for b, cross in zip(index, [product(1, b, 0) for b in index]):
            keep(gram, NEXT_PITCH, b, cross)

    def gram_own(index):
        for b in index:
            sega[b] = jnp.concatenate(of_bin(1, b), 0).astype(jnp.bfloat16).T
        for b, cross in zip(index, [product(0, b, 0) for b in index]):
            keep(bins, BIN_PITCH, b, cross)

    tall = width - NO_FAR
    same = lax.broadcasted_iota(jnp.int32, (tall, width), 1)
    same = same > lax.broadcasted_iota(jnp.int32, (tall, width), 0) + NO_FAR

    def gram_far(index):
        crosses = [product(1, b, NO_FAR) for b in index]
        places = [pl.ds((2 * b + h) * BIN_PITCH + NO_FAR, tall) for b in index for h in range(2)]
        before = [bins[place, :] for place in places]
        for e, place in enumerate(places):
            h = e % 2
            cross = crosses[e // 2][:, h * width : (h + 1) * width]
            bins[place, :] = jnp.where(same, before[e], cross)

    def place_next(ahead, c):
        return width + ahead - c

    def place_own(ahead, c):
        return jnp.where(ahead + 7 > c, ahead - c, 2 * width + ahead - c)

    def lag_step(source, pitch, place, base):
        def step(index):
            cross = jnp.concatenate(
                [
                    source[pl.ds(base + c, 2 * BINS, stride=pitch), :].astype(jnp.bfloat16)
                    for c in index
                ],
                1,
            )
            lags = lax.dot_general(
                cross, lag[...], (((0,), (0,)), ((), ())), preferred_element_type=jnp.float32
            )
            for u, c in enumerate(index):
                for e in range(width // 8):
                    k = jnp.clip(place(8 * e, base + c), -FIRST, BAND + 1)
                    at = u * width + 8 * e
                    first = (k + FIRST) * ROW_PITCH + c
                    rows[pl.ds(first, 8, stride=ROW_PITCH), :] = lags[at : at + 8]

        return step

    done = MID
    for c in range(PIECES):
        tables[c].wait()
        halves = []
        for parity in range(2):
            total = jnp.zeros((piece, 2 * width), jnp.float32)
            for p in range(parity * KEPT // 128, (parity + 1) * KEPT // 128, 2):
                first = c % 2 * area + p * piece
                block = jnp.concatenate(
                    [part[first : first + piece, :], part[first + piece : first + 2 * piece, :]], 1
                )
                total += jnp.dot(
                    block, white[p * 128 : (p + 2) * 128, :], preferred_element_type=jnp.float32
                )
            halves.append(total)
        if c + 2 < PIECES:
            tables[c + 2].start()
        first, end = c * piece, (c + 1) * piece
        kept = min(end, MID) - first
        ya[first : first + kept, :] = (halves[0] + halves[1])[:kept].astype(jnp.bfloat16)
        later = halves[0] - halves[1]
        for w in range(2):
            rows[w * BASE + first : w * BASE + end, :] = later[:, w * width : (w + 1) * width]
        ready = (end + SAMP // 2) // 16 * 16
        for w in range(2):
            source = slice(w * BASE + done - SAMP // 2, w * BASE + ready - SAMP // 2)
            ya[done:ready, w * width : (w + 1) * width] = rows[source, :].astype(jnp.bfloat16)
        done = ready
        if c == PIECES - 1:
            ya[done:, :] = jnp.zeros((SERIES - done, 2 * width), jnp.bfloat16)
        for h in range(2):
            to_near[2 * c + h].start()
        long_segments(turns_long[c])
        short_batch(own_block, 0, None, turns_short[c])

    unrolled(BINS, gram_own, 8)

    @pl.when(odd)
    def _():
        unrolled(SLOTS, pack_segments, 16)
        unrolled(EXTRA_ROWS // SEG, pack_extra, 6)

    for c in range(PIECES):
        for h in range(2):
            to_near[2 * c + h].wait_recv()
        if c == PIECES - 1:

            @pl.when(odd)
            def _():
                for copy in to_far:
                    copy.start()

        short_batch(near_block, 1, j == blocks - 1, turns_short[c])

    @pl.when(odd)
    def _():
        for copy in pass_on:
            copy.start()

    unrolled(BINS, gram_next, 8)

    def take_far():
        @pl.when(odd)
        def _():
            for copy in to_far:
                copy.wait_recv()

        @pl.when(jnp.logical_not(odd))
        def _():
            for copy in pass_on:
                copy.wait_recv()

        short_segments(far_block, 1, j >= blocks - 2)
        unrolled(BINS, gram_far, 8)

    def at(column, row):
        return row * RING + lax.rem(column + RING, RING)

    half = share // 2 + 1
    low, high, whole = (0, half), (half, share - half), (0, share)

    def spot(n, place, k, per):
        return pl.multiple_of(((n * per + place) * share + k) * CHUNK, CHUNK)

    def part_at(n, place, k=0, count=1):
        return pl.ds(spot(n, place, k, BAND // share), count * CHUNK)

    def inbox_at(n, place, k=0, count=1):
        return pl.ds(spot(n, place, k, BOXES), count * CHUNK)

    def message(n, m):
        def block(column, row, ks):
            return part.at[part_at(n, at(column, row), *ks)]

        def box(place, ks):
            return inbox.at[inbox_at(n, place, *ks)]

        if KINDS[n] == "X":
            source, target, device = [
                (block(x + 2, 0, whole), box(0, whole), right),
                (block(x + 2, 1, whole), box(1, whole), left),
                (block(x + 1, 1, whole), box(3, whole), right),
                (block(x - 1, 0, whole), box(4, whole), left),
                (block(x + 1, 0, whole), box(2, whole), right),
                (block(x - 1, 1, whole), box(5, whole), left),
                (block(x, 1 - z, whole), box(6, whole), other),
            ][m]
        else:
            four = (0, RING * share)
            source, target, device = [
                (part.at[part_at(n, (1 - z) * RING, *four)], box(0, four), other),
                (block(x + 2, z, low), box(4, low), right),
                (block(x + 2, z, high), box(4, high), left),
                (block(x + 1, z, high), box(5, high), right),
                (block(x - 1, z, low), box(6, low), left),
                (block(x + 1, z, low), box(5, low), right),
                (block(x - 1, z, high), box(6, high), left),
            ][m]
        return remote(source, target, sent.at[n, m], come.at[n, m], device)

    def start(n, *which):
        for m in which:
            message(n, m).start()

    def wait(n, *which):
        for m in which:
            message(n, m).wait_recv()

    def summed(n, place, boxes, k):
        total = part[part_at(n, place, k), :].astype(jnp.float32)
        for box in boxes:
            total += inbox[inbox_at(n, box, k), :].astype(jnp.float32)
        return total

    def plus(n, place, boxes, ks):
        first, count = ks

        def step(index):
            for k in index:
                total = summed(n, place, boxes, first + k)
                part[part_at(n, place, first + k), :] = total.astype(jnp.bfloat16)

        unrolled(count, step, 5 if count % 5 == 0 else count)

    def begin(n):
        unrolled(CHUNK, lag_step(gram, NEXT_PITCH, place_next, n * CHUNK), 8)
        unrolled(CHUNK, lag_step(bins, BIN_PITCH, place_own, n * CHUNK), 8)

        def step(index):
            for k in index:
                for d in range(BAND // share):
                    first = (d * share + k + FIRST + 1) * ROW_PITCH
                    part[part_at(n, d, k), :] = rows[pl.ds(first, CHUNK), :].astype(jnp.bfloat16)

        unrolled(share, step, 5)
        start(n, *((0, 1, 2, 3) if KINDS[n] == "X" else (0,)))

    def second(n):
        if KINDS[n] == "X":
            wait(n, 0, 1)
            plus(n, at(x + 1, 0), [0], whole)
            start(n, 4)
            plus(n, at(x - 1, 1), [1], whole)
            start(n, 5)
        else:
            wait(n, 0)
            for step in (2, 1, 3, 0):
                plus(n, at(x + step, z), [(x + step) % RING], whole)
                start(n, *{2: (1, 2), 1: (3,), 3: (4,), 0: ()}[step])

    def third(n):
        if KINDS[n] == "X":
            wait(n, 2, 3, 4, 5)
            plus(n, at(x, 1 - z), [3 - z, 5 - z], whole)
            start(n, 6)
        else:
            wait(n, 1, 2)
            plus(n, at(x + 1, z), [4], low)
            start(n, 5)
            plus(n, at(x - 1, z), [4], high)
            start(n, 6)

    def last(n):
        if KINDS[n] == "X":
            wait(n, 6)
            boxes = (2 + z, 4 + z, 6)
        else:
            wait(n, 3, 4, 5, 6)
            boxes = (5, 6)

        slot = n % 2
        if n in shown:
            shown[n].wait()

        def step(index):
            for k in index:
                stage[slot, k] = summed(n, at(x, z), boxes, k)

        unrolled(share, step, 5)
        result(n).start()
        for m in range(7):
            message(n, m).wait_send()

    def result(n):
        return pltpu.make_async_copy(
            stage.at[n % 2], out.at[:, pl.ds(n * CHUNK, CHUNK)], local.at[2 + n % 2]
        )

    order = [int(name[1:]) for name in STEPS if name[0] == "l"]
    shown, ending = {}, {}
    for n in order:
        if n % 2 in ending:
            shown[n] = result(ending[n % 2])
        ending[n % 2] = n
    stages = {"b": begin, "s": second, "t": third, "l": last}
    for name in STEPS:
        if name == "f":
            take_far()
        else:
            stages[name[0]](int(name[1:]))

    for n in ending.values():
        result(n).wait()
    for copy in to_near:
        copy.wait_send()

    @pl.when(odd)
    def _():
        for copy in to_far + pass_on:
            copy.wait_send()


def correlate(white, windows, groups):
    width = white.shape[1] // 2
    share = BAND // groups
    chunks = width // CHUNK
    fa, fd = segment_tables()
    vmem = pl.BlockSpec(memory_space=pltpu.VMEM)
    hbm = pl.BlockSpec(memory_space=pl.ANY)
    block = share * CHUNK
    return pl.pallas_call(
        pair_kernel,
        out_shape=jax.ShapeDtypeStruct((share, width, LAGS), jnp.float32),
        in_specs=[vmem, hbm, vmem, vmem, vmem],
        out_specs=hbm,
        scratch_shapes=[
            pltpu.VMEM((BINS, width, HELD), jnp.bfloat16),
            pltpu.VMEM((2 * BINS * BIN_PITCH, width), jnp.float32),
            pltpu.VMEM((2 * BINS * NEXT_PITCH, width), jnp.float32),
            pltpu.VMEM((OUT_ROWS * ROW_PITCH, LAGS), jnp.float32),
            pltpu.VMEM((SERIES, 2 * width), jnp.bfloat16),
            pltpu.VMEM((PAD, 2 * width), jnp.bfloat16),
            pltpu.VMEM((PAD, width), jnp.bfloat16),
            pltpu.VMEM((EXTRA_ROWS, width), jnp.bfloat16),
            pltpu.VMEM((2, PAD, width), jnp.bfloat16),
            pltpu.VMEM((chunks * groups * block, LAGS), jnp.bfloat16),
            pltpu.VMEM((chunks * BOXES * block, LAGS), jnp.bfloat16),
            pltpu.VMEM((2, share, CHUNK, LAGS), jnp.float32),
            pltpu.SemaphoreType.DMA((chunks, 7)),
            pltpu.SemaphoreType.DMA((chunks, 7)),
            pltpu.SemaphoreType.DMA((2 * PIECES + 4,)),
            pltpu.SemaphoreType.DMA((2 * PIECES + 2,)),
            pltpu.SemaphoreType.DMA((4,)),
        ],
        compiler_params=pltpu.CompilerParams(
            vmem_limit_bytes=63 * 2**20, collective_id=0, has_side_effects=True
        ),
        cost_estimate=pl.CostEstimate(flops=6 * 10**9, bytes_accessed=24 * 10**6, transcendentals=0),
    )(
        white,
        jnp.asarray(inverse_table()),
        jnp.asarray(fa),
        jnp.asarray(fd),
        jnp.asarray(lag_table(windows)),
    )


def body(record, starts):
    groups = lax.axis_size("tm")
    white = whitened(record, starts)
    return correlate(white, starts.shape[0] * groups, groups)


def solution(mesh):
    return jax.shard_map(
        body,
        mesh=mesh,
        in_specs=(P("tm", "chan"), P("tm")),
        out_specs=P("tm", "chan", None),
        check_vma=False,
    )
```

```python
import functools
import math

import jax
import jax.numpy as jnp
import ml_dtypes
import numpy as np
from jax import lax
from jax.experimental import pallas as pl
from jax.experimental.pallas import tpu as pltpu
from jax.sharding import PartitionSpec as P

SAMP = 3000
F = 1501
PAD = 3072
KEPT = PAD // 2
GROUP = 384
PIECES = 4
BASE = 1664
MID = 1600
BAND = 200
LAGS = 128
HALF = LAGS // 2
SEG = 64
SLOTS = 48
FULL = SAMP // SEG
SPAN = 192
POINTS = 191
BINS = 96
SERIES = SEG * (SLOTS + 2)
BF16 = ml_dtypes.bfloat16


def turns(a, b, period):
    return 2.0 * math.pi * (np.outer(a, b) % period) / period


def bins_of(parity, reverse):
    bins = 2 * np.arange(GROUP) + parity
    bins[bins > F // 2 + 1] = -1
    if reverse:
        bins = np.where(bins >= 0, F - 1 - bins, -1)
        bins[bins <= F // 2] = -1
    else:
        bins[bins > F // 2] = -1
    return bins


def dft_table():
    table = np.zeros((2, 2, GROUP, 2, KEPT), np.float32)
    for parity in range(2):
        bins = np.arange(parity, F // 2 + 2, 2)
        for late in range(2):
            angle = turns(bins, np.arange(late, SAMP, 2), SAMP)
            table[parity, 0, : len(bins), late, : SAMP // 2] = np.cos(angle) / math.sqrt(SAMP)
            table[parity, 1, : len(bins), late, : SAMP // 2] = -np.sin(angle) / math.sqrt(SAMP)
    return table.reshape(KEPT, PAD).astype(BF16)


def inverse_table():
    time = (np.arange(BASE) - HALF) % SAMP
    table = np.zeros((BASE, 2, 2, 2, GROUP), np.float32)
    for parity in range(2):
        for reverse in range(2):
            bins = bins_of(parity, reverse)
            weight = np.where(bins < 0, 0.0, np.where((bins == 0) | (bins == F - 1), 1.0, 2.0))
            weight /= math.sqrt(SAMP)
            angle = turns(time, np.maximum(bins, 0), SAMP)
            table[:, parity, reverse, 0] = weight * np.cos(angle)
            table[:, parity, reverse, 1] = -weight * np.sin(angle)
    table = table.reshape(PIECES, BASE // PIECES, PAD // 128, 128)
    return np.moveaxis(table, 2, 1).reshape(-1, 128).astype(BF16)


def segment_tables():
    angle = turns(np.arange(BINS), np.arange(SPAN), POINTS)
    full = np.stack([np.cos(angle), -np.sin(angle)], axis=1) / math.sqrt(POINTS)
    full = full.reshape(2 * BINS, SPAN)
    full[:, POINTS:] = 0.0
    high = full.astype(BF16)
    low = (full - high.astype(np.float64)).astype(BF16)
    short = np.stack([high[:, :SEG], low[:, :SEG]])
    short = np.stack([short, np.zeros_like(short), short])
    short[2, :, :, SAMP % SEG :] = 0.0
    return high, np.concatenate([short[:, 0], short[:, 1]], axis=2)


def lag_table(windows):
    angle = turns(np.arange(BINS), np.arange(LAGS), POINTS)
    weight = np.full((BINS, 1), 2.0)
    weight[0] = 1.0
    table = np.stack([weight * np.cos(angle), -weight * np.sin(angle)], axis=1)
    return (table / math.sqrt(SAMP * windows)).reshape(2 * BINS, LAGS).astype(BF16)


TALL = 3024
EDGE = 8


def white_kernel(starts, record, table, white, held, raw, wide, samples, spec, power, sems, wins):
    width = record.shape[1]
    loads, shifts = [], []
    for w in range(2):
        base = jnp.minimum(starts[w] // 16 * 16, record.shape[0] - TALL)
        shifts.append(starts[w] - base)
        base = pl.multiple_of(base, 16)
        loads.append(
            pltpu.make_async_copy(record.at[pl.ds(base, TALL)], raw.at[w], wins.at[w])
        )
        loads[w].start()
    pieces = [
        pltpu.make_async_copy(
            table.at[pl.ds(i * 2 * GROUP, 2 * GROUP)], held.at[pl.ds(i * 2 * GROUP, 2 * GROUP)],
            sems.at[i],
        )
        for i in range(2)
    ]
    pieces[0].start()
    zero = jnp.zeros((EDGE, 2 * width), jnp.float32)
    for parity in range(2):
        for h in range(2):
            power[parity, h, :EDGE, :] = zero
            power[parity, h, EDGE + GROUP :, :] = zero
    for w in range(2):
        loads[w].wait()
        wide[w, :TALL, :] = raw[w].astype(jnp.float32)
        wide[w, TALL:, :] = jnp.zeros((wide.shape[1] - TALL, width), jnp.float32)
        for late in range(2):
            samples[late, :, w * width : (w + 1) * width] = wide[
                w, pl.ds(shifts[w] + late, KEPT, stride=2), :
            ].astype(jnp.bfloat16)

    def group(parity, h, ri):
        first = (parity * 4 + h * 2 + ri) * GROUP
        return slice(first, first + GROUP)

    for parity in range(2):
        pieces[parity].wait()
        if parity == 0:
            pieces[1].start()
        part = slice(parity * 2 * GROUP, (parity + 1) * 2 * GROUP)
        early, late = [
            jnp.dot(
                held[part, e * KEPT : (e + 1) * KEPT], samples[e],
                preferred_element_type=jnp.float32,
            )
            for e in range(2)
        ]
        for ri in range(2):
            one, two = [found[ri * GROUP : (ri + 1) * GROUP] for found in (early, late)]
            spec[group(parity, 0, ri), :] = one + two
            spec[group(parity, 1, ri), :] = two - one if ri else one - two
        for h in range(2):
            real, imag = [spec[group(parity, h, ri), :] for ri in range(2)]
            power[parity, h, EDGE : EDGE + GROUP, :] = real * real + imag * imag

    for parity in range(2):
        for h in range(2):
            for first in range(0, GROUP, 128):
                at = EDGE + first
                beside = (at, at + 1) if parity else (at - 1, at)
                smooth = power[parity, h, at : at + 128, :]
                for place in beside:
                    smooth = smooth + power[1 - parity, h, place : place + 128, :]
                factor = 1.0 / jnp.maximum(jnp.sqrt(smooth / 3.0), 0.5)
                for ri in range(2):
                    start = group(parity, h, ri).start + first
                    part = slice(start, start + 128)
                    white[part, :] = (spec[part, :] * factor).astype(jnp.bfloat16)


def whitened(record, starts):
    width = record.shape[1]
    return pl.pallas_call(
        white_kernel,
        out_shape=jax.ShapeDtypeStruct((PAD, 2 * width), jnp.bfloat16),
        in_specs=[
            pl.BlockSpec(memory_space=pltpu.SMEM),
            pl.BlockSpec(memory_space=pl.ANY),
            pl.BlockSpec(memory_space=pl.ANY),
        ],
        out_specs=pl.BlockSpec(memory_space=pltpu.VMEM),
        scratch_shapes=[
            pltpu.VMEM((KEPT, PAD), jnp.bfloat16),
            pltpu.VMEM((2, TALL, width), jnp.bfloat16),
            pltpu.VMEM((2, PAD + 32, width), jnp.float32),
            pltpu.VMEM((2, KEPT, 2 * width), jnp.bfloat16),
            pltpu.VMEM((PAD, 2 * width), jnp.float32),
            pltpu.VMEM((2, 2, GROUP + 2 * EDGE, 2 * width), jnp.float32),
            pltpu.SemaphoreType.DMA((PIECES,)),
            pltpu.SemaphoreType.DMA((2,)),
        ],
        compiler_params=pltpu.CompilerParams(vmem_limit_bytes=62 * 2**20),
        cost_estimate=pl.CostEstimate(
            flops=5 * 10**9, bytes_accessed=22 * 10**6, transcendentals=400_000
        ),
    )(starts, record, jnp.asarray(dft_table()))


FIRST = 8
OUT_ROWS = FIRST + BAND + 9
HELD = 2 * 2 * SLOTS
CHUNK = 16
BOXES = 7
RING = 4
BIN_PITCH = 225
NEXT_PITCH = 129
ROW_PITCH = 17
SECOND = 128
EXTRA = 8
EXTRA_ROWS = 384
NO_FAR = 48
KINDS = "XXZXZXXZ"
STEPS = (
    "b0", "b1", "b2", "s0", "f", "t0", "s1", "s2", "b3", "b4", "t1",
    "t2", "b5", "b6", "s3", "b7", "l0", "l2", "s5", "s4", "l1", "s6",
    "t3", "t5", "s7", "t4", "l3", "t6", "l5", "t7", "l4", "l6", "l7",
)
MESH = pl.DeviceIdType.MESH


def unrolled(count, step, times):
    def several(i, carry):
        step([i * times + u for u in range(times)])
        return carry

    lax.fori_loop(0, count // times, several, 0)


def pair_kernel(
    white, inverse, fa, fd, lag, out,
    sega, bins, gram, rows, ya, near, pack, extra, far, part, inbox, stage,
    sent, come, sent_y, come_y, local,
):
    width = out.shape[1]
    share = out.shape[0]
    blocks = lax.axis_size("chan")
    i, j = lax.axis_index("tm"), lax.axis_index("chan")
    x, z = lax.rem(i, RING), i // RING
    right = {"tm": z * RING + lax.rem(x + 1, RING)}
    left = {"tm": z * RING + lax.rem(x + RING - 1, RING)}
    other = {"tm": (1 - z) * RING + x}
    odd = lax.rem(j, 2) == 1

    def behind(distance):
        return {"chan": lax.rem(j + blocks + distance, blocks)}

    piece = BASE // PIECES
    area = piece * (PAD // 128)
    tables = [
        pltpu.make_async_copy(
            inverse.at[pl.ds(c * area, area)], part.at[pl.ds(c % 2 * area, area)], local.at[c % 2]
        )
        for c in range(PIECES)
    ]
    tables[0].start()
    tables[1].start()

    barrier = pltpu.get_barrier_semaphore()
    peers = (right, left, other, behind(-1), behind(1), behind(-2), behind(2))
    for device in peers:
        pl.semaphore_signal(barrier, inc=1, device_id=device, device_id_type=MESH)
    pl.semaphore_wait(barrier, len(peers))

    def remote(source, target, send, receive, device):
        return pltpu.make_async_remote_copy(
            src_ref=source, dst_ref=target, send_sem=send, recv_sem=receive,
            device_id=device, device_id_type=MESH,
        )

    spans, turns_long, turns_short = [], [], []
    done, began, fresh = MID, (0, MID // SEG), (0, MID // SEG - 1)
    for c in range(PIECES):
        first, end = c * piece, (c + 1) * piece
        ready = (end + SAMP // 2) // 16 * 16
        low_end = min(end, MID)
        spans.append(((max(first, SEG), low_end), (done, min(ready, SEG * SLOTS))))
        done = ready
        final = c == PIECES - 1
        stop = (
            MID // SEG if final else (end - SPAN) // SEG + 1,
            SLOTS if final else (ready - SPAN) // SEG + 1,
        )
        turns_long.append([s for h in range(2) for s in range(began[h], stop[h])])
        began = stop
        stop = (
            MID // SEG - 1 if final else end // SEG - 1,
            SLOTS if final else ready // SEG - 1,
        )
        turns_short.append([s for h in range(2) for s in range(fresh[h], stop[h])])
        fresh = stop
    parts = 2 * PIECES
    to_near = [
        remote(
            ya.at[pl.ds(first, end - first)], near.at[pl.ds(first - SEG, end - first)],
            sent_y.at[2 * c + h], come_y.at[2 * c + h], behind(-1),
        )
        for c in range(PIECES)
        for h, (first, end) in enumerate(spans[c])
    ]
    to_far = [
        remote(pack, far.at[0], sent_y.at[parts], come_y.at[parts], behind(-2)),
        remote(
            extra, far.at[1, pl.ds(0, EXTRA_ROWS)],
            sent_y.at[parts + 1], come_y.at[parts + 1], behind(-2),
        ),
    ]
    pass_on = [
        remote(
            near.at[:, pl.ds(w * width, width)], far.at[w],
            sent_y.at[parts + 2 + w], come_y.at[parts + w], behind(-1),
        )
        for w in range(2)
    ]

    has_near, has_far = j < blocks - 1, j < blocks - 2
    near[SEG * (SLOTS - 1) :, :] = jnp.zeros((SEG, 2 * width), jnp.bfloat16)

    @pl.when(jnp.logical_not(has_near))
    def _():
        near[: SEG * (SLOTS - 1), :] = jnp.zeros((SEG * (SLOTS - 1), 2 * width), jnp.bfloat16)

    @pl.when(jnp.logical_not(has_far))
    def _():
        far[...] = jnp.zeros(far.shape, jnp.bfloat16)

    lane = lax.broadcasted_iota(jnp.int32, (SEG, width), 1)
    def pack_segments(index):
        for s in index:
            block = ya[pl.ds(pl.multiple_of((s + 1) * SEG, SEG), SEG), :].astype(jnp.float32)
            turned = pltpu.roll(block[:, width:], width // 2, 1)
            pack[pl.ds(pl.multiple_of(s * SEG, SEG), SEG), :] = jnp.where(
                lane < width // 2, block[:, :width], turned
            ).astype(jnp.bfloat16)

    def pack_extra(index):
        for e in index:
            total = jnp.zeros((SEG, width), jnp.float32)
            for g in range(PAD // EXTRA_ROWS):
                first = pl.multiple_of((e + 1) * SEG, SEG) + g * EXTRA_ROWS
                block = ya[pl.ds(first, SEG), :].astype(jnp.float32)
                for w in range(2):
                    place = (2 * g + w) * EXTRA
                    turned = pltpu.roll(
                        block[:, w * width : (w + 1) * width], (place + width // 2) % width, 1
                    )
                    total = jnp.where((lane >= place) & (lane < place + EXTRA), turned, total)
            extra[pl.ds(pl.multiple_of(e * SEG, SEG), SEG), :] = total.astype(jnp.bfloat16)

    def far_block(s):
        group, row = s // (EXTRA_ROWS // SEG), lax.rem(s, EXTRA_ROWS // SEG)
        first = far[0, pl.ds(pl.multiple_of(s * SEG, SEG), SEG), :].astype(jnp.float32)
        row = jnp.where(odd, row, s)
        rest = far[1, pl.ds(pl.multiple_of(row * SEG, SEG), SEG), :].astype(jnp.float32)
        half = width // 2
        both = []
        for w in range(2):
            body = first if w == 0 else pltpu.roll(first, half, 1)
            turn = lax.rem(half + width - (2 * group + w) * EXTRA, width)
            both.append(jnp.where(lane < half, body, pltpu.roll(rest, turn, 1)))
        block = jnp.concatenate(
            [jnp.where(odd, both[0], first), jnp.where(odd, both[1], rest)], 1
        )
        return block.astype(jnp.bfloat16)

    def spread(slot, s, spec):
        at = slot * SECOND + s
        bins[pl.ds(at, 2 * BINS, stride=BIN_PITCH), :] = spec[:, :width]
        bins[pl.ds(at + SLOTS, 2 * BINS, stride=BIN_PITCH), :] = spec[:, width:]

    def long_segments(index):
        specs = []
        for s in index:
            block = ya[s * SEG : s * SEG + SPAN, :]
            specs.append(jnp.dot(fa[...], block, preferred_element_type=jnp.float32))
        for s, spec in zip(index, specs):
            spread(1, s, spec)

    def short_batch(block_of, slot, absent, index):
        specs = []
        for s in index:
            block = block_of(s)
            twice = jnp.concatenate([block, block], 0)
            if isinstance(s, int):
                kind = 0 if s < FULL else 2 if s == FULL else 1
            else:
                kind = jnp.where(s < FULL, 0, jnp.where(s == FULL, 2, 1))
            if absent is not None:
                kind = jnp.where(absent, 1, kind)
            specs.append(jnp.dot(fd[kind], twice, preferred_element_type=jnp.float32))
        for s, spec in zip(index, specs):
            spread(slot, s, spec)

    def short_segments(block_of, slot, absent):
        unrolled(SLOTS, functools.partial(short_batch, block_of, slot, absent), 8)

    def place_of(s):
        return s * SEG if isinstance(s, int) else pl.multiple_of(s * SEG, SEG)

    def own_block(s):
        return ya[pl.ds(place_of(s + 1), SEG), :]

    def near_block(s):
        return near[pl.ds(place_of(s), SEG), :]

    def of_bin(slot, b):
        first = b * 2 * BIN_PITCH + slot * SECOND
        return bins[pl.ds(first, 2 * SLOTS), :], bins[pl.ds(first + BIN_PITCH, 2 * SLOTS), :]

    def product(slot, b, first):
        real, imag = [part.astype(jnp.bfloat16) for part in of_bin(slot, b)]
        both = jnp.concatenate(
            [jnp.concatenate([real, imag], 0), jnp.concatenate([-imag, real], 0)], 1
        )
        return jnp.dot(sega[b, first:, :], both, preferred_element_type=jnp.float32)

    def keep(target, pitch, b, cross):
        first = b * 2 * pitch
        target[pl.ds(first, width), :] = cross[:, :width]
        target[pl.ds(first + pitch, width), :] = cross[:, width:]

    def gram_next(index):
        for b, cross in zip(index, [product(1, b, 0) for b in index]):
            keep(gram, NEXT_PITCH, b, cross)

    def gram_own(index):
        for b in index:
            sega[b] = jnp.concatenate(of_bin(1, b), 0).astype(jnp.bfloat16).T
        for b, cross in zip(index, [product(0, b, 0) for b in index]):
            keep(bins, BIN_PITCH, b, cross)

    tall = width - NO_FAR
    same = lax.broadcasted_iota(jnp.int32, (tall, width), 1)
    same = same > lax.broadcasted_iota(jnp.int32, (tall, width), 0) + NO_FAR

    def gram_far(index):
        crosses = [product(1, b, NO_FAR) for b in index]
        places = [pl.ds((2 * b + h) * BIN_PITCH + NO_FAR, tall) for b in index for h in range(2)]
        before = [bins[place, :] for place in places]
        for e, place in enumerate(places):
            h = e % 2
            cross = crosses[e // 2][:, h * width : (h + 1) * width]
            bins[place, :] = jnp.where(same, before[e], cross)

    def place_next(ahead, c):
        return width + ahead - c

    def place_own(ahead, c):
        return jnp.where(ahead + 7 > c, ahead - c, 2 * width + ahead - c)

    def lag_step(source, pitch, place, base):
        def step(index):
            cross = jnp.concatenate(
                [
                    source[pl.ds(base + c, 2 * BINS, stride=pitch), :].astype(jnp.bfloat16)
                    for c in index
                ],
                1,
            )
            lags = lax.dot_general(
                cross, lag[...], (((0,), (0,)), ((), ())), preferred_element_type=jnp.float32
            )
            for u, c in enumerate(index):
                for e in range(width // 8):
                    k = jnp.clip(place(8 * e, base + c), -FIRST, BAND + 1)
                    at = u * width + 8 * e
                    first = (k + FIRST) * ROW_PITCH + c
                    rows[pl.ds(first, 8, stride=ROW_PITCH), :] = lags[at : at + 8]

        return step

    done = MID
    for c in range(PIECES):
        tables[c].wait()
        halves = []
        for parity in range(2):
            total = jnp.zeros((piece, 2 * width), jnp.float32)
            for p in range(parity * KEPT // 128, (parity + 1) * KEPT // 128, 2):
                first = c % 2 * area + p * piece
                block = jnp.concatenate(
                    [part[first : first + piece, :], part[first + piece : first + 2 * piece, :]], 1
                )
                total += jnp.dot(
                    block, white[p * 128 : (p + 2) * 128, :], preferred_element_type=jnp.float32
                )
            halves.append(total)
        if c + 2 < PIECES:
            tables[c + 2].start()
        first, end = c * piece, (c + 1) * piece
        kept = min(end, MID) - first
        ya[first : first + kept, :] = (halves[0] + halves[1])[:kept].astype(jnp.bfloat16)
        later = halves[0] - halves[1]
        for w in range(2):
            rows[w * BASE + first : w * BASE + end, :] = later[:, w * width : (w + 1) * width]
        ready = (end + SAMP // 2) // 16 * 16
        for w in range(2):
            source = slice(w * BASE + done - SAMP // 2, w * BASE + ready - SAMP // 2)
            ya[done:ready, w * width : (w + 1) * width] = rows[source, :].astype(jnp.bfloat16)
        done = ready
        if c == PIECES - 1:
            ya[done:, :] = jnp.zeros((SERIES - done, 2 * width), jnp.bfloat16)

        @pl.when(j > 0)
        def _():
            for h in range(2):
                to_near[2 * c + h].start()

        long_segments(turns_long[c])
        short_batch(own_block, 0, None, turns_short[c])

    unrolled(BINS, gram_own, 8)

    @pl.when(odd)
    def _():
        unrolled(SLOTS, pack_segments, 16)
        unrolled(EXTRA_ROWS // SEG, pack_extra, 6)

    for c in range(PIECES):

        @pl.when(has_near)
        def _():
            for h in range(2):
                to_near[2 * c + h].wait_recv()

        if c == PIECES - 1:

            @pl.when(odd & (j > 1))
            def _():
                for copy in to_far:
                    copy.start()

        short_batch(near_block, 1, j == blocks - 1, turns_short[c])

    @pl.when(odd & has_near)
    def _():
        for copy in pass_on:
            copy.start()

    unrolled(BINS, gram_next, 8)

    def take_far():
        @pl.when(odd & has_far)
        def _():
            for copy in to_far:
                copy.wait_recv()

        @pl.when(jnp.logical_not(odd) & has_far)
        def _():
            for copy in pass_on:
                copy.wait_recv()

        short_segments(far_block, 1, j >= blocks - 2)
        unrolled(BINS, gram_far, 8)

    def at(column, row):
        return row * RING + lax.rem(column + RING, RING)

    half = share // 2 + 1
    low, high, whole = (0, half), (half, share - half), (0, share)

    def spot(n, place, k, per):
        return pl.multiple_of(((n * per + place) * share + k) * CHUNK, CHUNK)

    def part_at(n, place, k=0, count=1):
        return pl.ds(spot(n, place, k, BAND // share), count * CHUNK)

    def inbox_at(n, place, k=0, count=1):
        return pl.ds(spot(n, place, k, BOXES), count * CHUNK)

    def message(n, m):
        def block(column, row, ks):
            return part.at[part_at(n, at(column, row), *ks)]

        def box(place, ks):
            return inbox.at[inbox_at(n, place, *ks)]

        if KINDS[n] == "X":
            source, target, device = [
                (block(x + 2, 0, whole), box(0, whole), right),
                (block(x + 2, 1, whole), box(1, whole), left),
                (block(x + 1, 1, whole), box(3, whole), right),
                (block(x - 1, 0, whole), box(4, whole), left),
                (block(x + 1, 0, whole), box(2, whole), right),
                (block(x - 1, 1, whole), box(5, whole), left),
                (block(x, 1 - z, whole), box(6, whole), other),
            ][m]
        else:
            four = (0, RING * share)
            source, target, device = [
                (part.at[part_at(n, (1 - z) * RING, *four)], box(0, four), other),
                (block(x + 2, z, low), box(4, low), right),
                (block(x + 2, z, high), box(4, high), left),
                (block(x + 1, z, high), box(5, high), right),
                (block(x - 1, z, low), box(6, low), left),
                (block(x + 1, z, low), box(5, low), right),
                (block(x - 1, z, high), box(6, high), left),
            ][m]
        return remote(source, target, sent.at[n, m], come.at[n, m], device)

    def start(n, *which):
        for m in which:
            message(n, m).start()

    def wait(n, *which):
        for m in which:
            message(n, m).wait_recv()

    def summed(n, place, boxes, k):
        total = part[part_at(n, place, k), :].astype(jnp.float32)
        for box in boxes:
            total += inbox[inbox_at(n, box, k), :].astype(jnp.float32)
        return total

    def plus(n, place, boxes, ks):
        first, count = ks

        def step(index):
            for k in index:
                total = summed(n, place, boxes, first + k)
                part[part_at(n, place, first + k), :] = total.astype(jnp.bfloat16)

        unrolled(count, step, 5 if count % 5 == 0 else count)

    def begin(n):
        unrolled(CHUNK, lag_step(gram, NEXT_PITCH, place_next, n * CHUNK), 8)
        unrolled(CHUNK, lag_step(bins, BIN_PITCH, place_own, n * CHUNK), 8)

        def step(index):
            for k in index:
                for d in range(BAND // share):
                    first = (d * share + k + FIRST + 1) * ROW_PITCH
                    part[part_at(n, d, k), :] = rows[pl.ds(first, CHUNK), :].astype(jnp.bfloat16)

        unrolled(share, step, 5)
        start(n, *((0, 1, 2, 3) if KINDS[n] == "X" else (0,)))

    def second(n):
        if KINDS[n] == "X":
            wait(n, 0, 1)
            plus(n, at(x + 1, 0), [0], whole)
            start(n, 4)
            plus(n, at(x - 1, 1), [1], whole)
            start(n, 5)
        else:
            wait(n, 0)
            for step in (2, 1, 3, 0):
                plus(n, at(x + step, z), [(x + step) % RING], whole)
                start(n, *{2: (1, 2), 1: (3,), 3: (4,), 0: ()}[step])

    def third(n):
        if KINDS[n] == "X":
            wait(n, 2, 3, 4, 5)
            plus(n, at(x, 1 - z), [3 - z, 5 - z], whole)
            start(n, 6)
        else:
            wait(n, 1, 2)
            plus(n, at(x + 1, z), [4], low)
            start(n, 5)
            plus(n, at(x - 1, z), [4], high)
            start(n, 6)

    def last(n):
        if KINDS[n] == "X":
            wait(n, 6)
            boxes = (2 + z, 4 + z, 6)
        else:
            wait(n, 3, 4, 5, 6)
            boxes = (5, 6)

        slot = n % 2
        if n in shown:
            shown[n].wait()

        def step(index):
            for k in index:
                stage[slot, k] = summed(n, at(x, z), boxes, k)

        unrolled(share, step, 5)
        result(n).start()
        for m in range(7):
            message(n, m).wait_send()

    def result(n):
        return pltpu.make_async_copy(
            stage.at[n % 2], out.at[:, pl.ds(n * CHUNK, CHUNK)], local.at[2 + n % 2]
        )

    order = [int(name[1:]) for name in STEPS if name[0] == "l"]
    shown, ending = {}, {}
    for n in order:
        if n % 2 in ending:
            shown[n] = result(ending[n % 2])
        ending[n % 2] = n
    stages = {"b": begin, "s": second, "t": third, "l": last}
    for name in STEPS:
        if name == "f":
            take_far()
        else:
            stages[name[0]](int(name[1:]))

    for n in ending.values():
        result(n).wait()

    @pl.when(j > 0)
    def _():
        for copy in to_near:
            copy.wait_send()

    @pl.when(odd & (j > 1))
    def _():
        for copy in to_far:
            copy.wait_send()

    @pl.when(odd & has_near)
    def _():
        for copy in pass_on:
            copy.wait_send()


def correlate(white, windows, groups):
    width = white.shape[1] // 2
    share = BAND // groups
    chunks = width // CHUNK
    fa, fd = segment_tables()
    vmem = pl.BlockSpec(memory_space=pltpu.VMEM)
    hbm = pl.BlockSpec(memory_space=pl.ANY)
    block = share * CHUNK
    return pl.pallas_call(
        pair_kernel,
        out_shape=jax.ShapeDtypeStruct((share, width, LAGS), jnp.float32),
        in_specs=[vmem, hbm, vmem, vmem, vmem],
        out_specs=hbm,
        scratch_shapes=[
            pltpu.VMEM((BINS, width, HELD), jnp.bfloat16),
            pltpu.VMEM((2 * BINS * BIN_PITCH, width), jnp.float32),
            pltpu.VMEM((2 * BINS * NEXT_PITCH, width), jnp.float32),
            pltpu.VMEM((OUT_ROWS * ROW_PITCH, LAGS), jnp.float32),
            pltpu.VMEM((SERIES, 2 * width), jnp.bfloat16),
            pltpu.VMEM((PAD, 2 * width), jnp.bfloat16),
            pltpu.VMEM((PAD, width), jnp.bfloat16),
            pltpu.VMEM((EXTRA_ROWS, width), jnp.bfloat16),
            pltpu.VMEM((2, PAD, width), jnp.bfloat16),
            pltpu.VMEM((chunks * groups * block, LAGS), jnp.bfloat16),
            pltpu.VMEM((chunks * BOXES * block, LAGS), jnp.bfloat16),
            pltpu.VMEM((2, share, CHUNK, LAGS), jnp.float32),
            pltpu.SemaphoreType.DMA((chunks, 7)),
            pltpu.SemaphoreType.DMA((chunks, 7)),
            pltpu.SemaphoreType.DMA((2 * PIECES + 4,)),
            pltpu.SemaphoreType.DMA((2 * PIECES + 2,)),
            pltpu.SemaphoreType.DMA((4,)),
        ],
        compiler_params=pltpu.CompilerParams(
            vmem_limit_bytes=63 * 2**20, collective_id=0, has_side_effects=True
        ),
        cost_estimate=pl.CostEstimate(flops=6 * 10**9, bytes_accessed=24 * 10**6, transcendentals=0),
    )(
        white,
        jnp.asarray(inverse_table()),
        jnp.asarray(fa),
        jnp.asarray(fd),
        jnp.asarray(lag_table(windows)),
    )


def body(record, starts):
    groups = lax.axis_size("tm")
    white = whitened(record, starts)
    return correlate(white, starts.shape[0] * groups, groups)


def solution(mesh):
    return jax.shard_map(
        body,
        mesh=mesh,
        in_specs=(P("tm", "chan"), P("tm")),
        out_specs=P("tm", "chan", None),
        check_vma=False,
    )
```

```python
import functools
import math

import jax
import jax.numpy as jnp
import ml_dtypes
import numpy as np
from jax import lax
from jax.experimental import pallas as pl
from jax.experimental.pallas import tpu as pltpu
from jax.sharding import PartitionSpec as P

SAMP = 3000
F = 1501
PAD = 3072
KEPT = PAD // 2
GROUP = 384
PIECES = 4
BASE = 1664
MID = 1600
BAND = 200
LAGS = 128
HALF = LAGS // 2
SEG = 64
SLOTS = 48
FULL = SAMP // SEG
SPAN = 192
POINTS = 191
BINS = 96
SERIES = SEG * (SLOTS + 2)
BF16 = ml_dtypes.bfloat16


def turns(a, b, period):
    return 2.0 * math.pi * (np.outer(a, b) % period) / period


def bins_of(parity, reverse):
    bins = 2 * np.arange(GROUP) + parity
    bins[bins > F // 2 + 1] = -1
    if reverse:
        bins = np.where(bins >= 0, F - 1 - bins, -1)
        bins[bins <= F // 2] = -1
    else:
        bins[bins > F // 2] = -1
    return bins


def dft_table():
    table = np.zeros((2, 2, GROUP, 2, KEPT), np.float32)
    for parity in range(2):
        bins = np.arange(parity, F // 2 + 2, 2)
        for late in range(2):
            angle = turns(bins, np.arange(late, SAMP, 2), SAMP)
            table[parity, 0, : len(bins), late, : SAMP // 2] = np.cos(angle) / math.sqrt(SAMP)
            table[parity, 1, : len(bins), late, : SAMP // 2] = -np.sin(angle) / math.sqrt(SAMP)
    return table.reshape(KEPT, PAD).astype(BF16)


def inverse_table():
    time = (np.arange(BASE) - HALF) % SAMP
    table = np.zeros((BASE, 2, 2, 2, GROUP), np.float32)
    for parity in range(2):
        for reverse in range(2):
            bins = bins_of(parity, reverse)
            weight = np.where(bins < 0, 0.0, np.where((bins == 0) | (bins == F - 1), 1.0, 2.0))
            weight /= math.sqrt(SAMP)
            angle = turns(time, np.maximum(bins, 0), SAMP)
            table[:, parity, reverse, 0] = weight * np.cos(angle)
            table[:, parity, reverse, 1] = -weight * np.sin(angle)
    table = table.reshape(PIECES, BASE // PIECES, PAD // 128, 128)
    return np.moveaxis(table, 2, 1).reshape(-1, 128).astype(BF16)


def segment_tables():
    angle = turns(np.arange(BINS), np.arange(SPAN), POINTS)
    full = np.stack([np.cos(angle), -np.sin(angle)], axis=1) / math.sqrt(POINTS)
    full = full.reshape(2 * BINS, SPAN)
    full[:, POINTS:] = 0.0
    high = full.astype(BF16)
    low = (full - high.astype(np.float64)).astype(BF16)
    short = np.stack([high[:, :SEG], low[:, :SEG]])
    short = np.stack([short, np.zeros_like(short), short])
    short[2, :, :, SAMP % SEG :] = 0.0
    return high, np.concatenate([short[:, 0], short[:, 1]], axis=2)


def lag_table(windows):
    angle = turns(np.arange(BINS), np.arange(LAGS), POINTS)
    weight = np.full((BINS, 1), 2.0)
    weight[0] = 1.0
    table = np.stack([weight * np.cos(angle), -weight * np.sin(angle)], axis=1)
    return (table / math.sqrt(SAMP * windows)).reshape(2 * BINS, LAGS).astype(BF16)


TALL = 3024
EDGE = 8


def white_kernel(starts, record, table, white, held, raw, wide, samples, spec, power, sems, wins):
    width = record.shape[1]
    loads, shifts = [], []
    for w in range(2):
        base = jnp.minimum(starts[w] // 16 * 16, record.shape[0] - TALL)
        shifts.append(starts[w] - base)
        base = pl.multiple_of(base, 16)
        loads.append(
            pltpu.make_async_copy(record.at[pl.ds(base, TALL)], raw.at[w], wins.at[w])
        )
        loads[w].start()
    pieces = [
        pltpu.make_async_copy(
            table.at[pl.ds(i * 2 * GROUP, 2 * GROUP)], held.at[pl.ds(i * 2 * GROUP, 2 * GROUP)],
            sems.at[i],
        )
        for i in range(2)
    ]
    pieces[0].start()
    zero = jnp.zeros((EDGE, 2 * width), jnp.float32)
    for parity in range(2):
        for h in range(2):
            power[parity, h, :EDGE, :] = zero
            power[parity, h, EDGE + GROUP :, :] = zero
    for w in range(2):
        loads[w].wait()
        wide[w, :TALL, :] = raw[w].astype(jnp.float32)
        wide[w, TALL:, :] = jnp.zeros((wide.shape[1] - TALL, width), jnp.float32)
        for late in range(2):
            samples[late, :, w * width : (w + 1) * width] = wide[
                w, pl.ds(shifts[w] + late, KEPT, stride=2), :
            ].astype(jnp.bfloat16)

    def group(parity, h, ri):
        first = (parity * 4 + h * 2 + ri) * GROUP
        return slice(first, first + GROUP)

    for parity in range(2):
        pieces[parity].wait()
        if parity == 0:
            pieces[1].start()
        part = slice(parity * 2 * GROUP, (parity + 1) * 2 * GROUP)
        early, late = [
            jnp.dot(
                held[part, e * KEPT : (e + 1) * KEPT], samples[e],
                preferred_element_type=jnp.float32,
            )
            for e in range(2)
        ]
        for ri in range(2):
            one, two = [found[ri * GROUP : (ri + 1) * GROUP] for found in (early, late)]
            spec[group(parity, 0, ri), :] = one + two
            spec[group(parity, 1, ri), :] = two - one if ri else one - two
        for h in range(2):
            real, imag = [spec[group(parity, h, ri), :] for ri in range(2)]
            power[parity, h, EDGE : EDGE + GROUP, :] = real * real + imag * imag

    for parity in range(2):
        for h in range(2):
            for first in range(0, GROUP, 128):
                at = EDGE + first
                beside = (at, at + 1) if parity else (at - 1, at)
                smooth = power[parity, h, at : at + 128, :]
                for place in beside:
                    smooth = smooth + power[1 - parity, h, place : place + 128, :]
                factor = 1.0 / jnp.maximum(jnp.sqrt(smooth / 3.0), 0.5)
                for ri in range(2):
                    start = group(parity, h, ri).start + first
                    part = slice(start, start + 128)
                    white[part, :] = (spec[part, :] * factor).astype(jnp.bfloat16)


def whitened(record, starts):
    width = record.shape[1]
    return pl.pallas_call(
        white_kernel,
        out_shape=jax.ShapeDtypeStruct((PAD, 2 * width), jnp.bfloat16),
        in_specs=[
            pl.BlockSpec(memory_space=pltpu.SMEM),
            pl.BlockSpec(memory_space=pl.ANY),
            pl.BlockSpec(memory_space=pl.ANY),
        ],
        out_specs=pl.BlockSpec(memory_space=pltpu.VMEM),
        scratch_shapes=[
            pltpu.VMEM((KEPT, PAD), jnp.bfloat16),
            pltpu.VMEM((2, TALL, width), jnp.bfloat16),
            pltpu.VMEM((2, PAD + 32, width), jnp.float32),
            pltpu.VMEM((2, KEPT, 2 * width), jnp.bfloat16),
            pltpu.VMEM((PAD, 2 * width), jnp.float32),
            pltpu.VMEM((2, 2, GROUP + 2 * EDGE, 2 * width), jnp.float32),
            pltpu.SemaphoreType.DMA((PIECES,)),
            pltpu.SemaphoreType.DMA((2,)),
        ],
        compiler_params=pltpu.CompilerParams(vmem_limit_bytes=62 * 2**20),
        cost_estimate=pl.CostEstimate(
            flops=5 * 10**9, bytes_accessed=22 * 10**6, transcendentals=400_000
        ),
    )(starts, record, jnp.asarray(dft_table()))


FIRST = 8
OUT_ROWS = FIRST + BAND + 9
HELD = 2 * 2 * SLOTS
CHUNK = 16
BOXES = 7
RING = 4
BIN_PITCH = 225
NEXT_PITCH = 129
ROW_PITCH = 17
SECOND = 128
EXTRA = 8
EXTRA_ROWS = 384
NO_FAR = 48
KINDS = "XXZXZXXZ"
STEPS = (
    "b0", "b1", "b2", "s0", "f", "t0", "s1", "s2", "b3", "b4", "t1",
    "t2", "b5", "b6", "s3", "b7", "l0", "l2", "s5", "s4", "l1", "s6",
    "t3", "t5", "s7", "t4", "l3", "t6", "l5", "t7", "l4", "l6", "l7",
)
MESH = pl.DeviceIdType.MESH


def unrolled(count, step, times):
    def several(i, carry):
        step([i * times + u for u in range(times)])
        return carry

    lax.fori_loop(0, count // times, several, 0)


def pair_kernel(
    white, inverse, fa, fd, lag, out,
    sega, bins, gram, rows, ya, near, pack, extra, far, part, inbox, stage,
    sent, come, sent_y, come_y, local,
):
    width = out.shape[1]
    share = out.shape[0]
    blocks = lax.axis_size("chan")
    i, j = lax.axis_index("tm"), lax.axis_index("chan")
    x, z = lax.rem(i, RING), i // RING
    right = {"tm": z * RING + lax.rem(x + 1, RING)}
    left = {"tm": z * RING + lax.rem(x + RING - 1, RING)}
    other = {"tm": (1 - z) * RING + x}
    odd = lax.rem(j, 2) == 1

    def behind(distance):
        return {"chan": lax.rem(j + blocks + distance, blocks)}

    piece = BASE // PIECES
    area = piece * (PAD // 128)
    tables = [
        pltpu.make_async_copy(
            inverse.at[pl.ds(c * area, area)], part.at[pl.ds(c % 2 * area, area)], local.at[c % 2]
        )
        for c in range(PIECES)
    ]
    tables[0].start()
    tables[1].start()

    barrier = pltpu.get_barrier_semaphore()
    peers = (right, left, other, behind(-1), behind(1), behind(-2), behind(2))
    for device in peers:
        pl.semaphore_signal(barrier, inc=1, device_id=device, device_id_type=MESH)

    def remote(source, target, send, receive, device):
        return pltpu.make_async_remote_copy(
            src_ref=source, dst_ref=target, send_sem=send, recv_sem=receive,
            device_id=device, device_id_type=MESH,
        )

    spans, turns_long, turns_short = [], [], []
    done, began, fresh = MID, (0, MID // SEG), (0, MID // SEG - 1)
    for c in range(PIECES):
        first, end = c * piece, (c + 1) * piece
        ready = (end + SAMP // 2) // 16 * 16
        low_end = min(end, MID)
        spans.append(((max(first, SEG), low_end), (done, min(ready, SEG * SLOTS))))
        done = ready
        final = c == PIECES - 1
        stop = (
            MID // SEG if final else (end - SPAN) // SEG + 1,
            SLOTS if final else (ready - SPAN) // SEG + 1,
        )
        turns_long.append([s for h in range(2) for s in range(began[h], stop[h])])
        began = stop
        stop = (
            MID // SEG - 1 if final else end // SEG - 1,
            SLOTS if final else ready // SEG - 1,
        )
        turns_short.append([s for h in range(2) for s in range(fresh[h], stop[h])])
        fresh = stop
    parts = 2 * PIECES
    to_near = [
        remote(
            ya.at[pl.ds(first, end - first)], near.at[pl.ds(first - SEG, end - first)],
            sent_y.at[2 * c + h], come_y.at[2 * c + h], behind(-1),
        )
        for c in range(PIECES)
        for h, (first, end) in enumerate(spans[c])
    ]
    to_far = [
        remote(pack, far.at[0], sent_y.at[parts], come_y.at[parts], behind(-2)),
        remote(
            extra, far.at[1, pl.ds(0, EXTRA_ROWS)],
            sent_y.at[parts + 1], come_y.at[parts + 1], behind(-2),
        ),
    ]
    pass_on = [
        remote(
            near.at[:, pl.ds(w * width, width)], far.at[w],
            sent_y.at[parts + 2 + w], come_y.at[parts + w], behind(-1),
        )
        for w in range(2)
    ]

    has_near, has_far = j < blocks - 1, j < blocks - 2
    near[SEG * (SLOTS - 1) :, :] = jnp.zeros((SEG, 2 * width), jnp.bfloat16)

    @pl.when(jnp.logical_not(has_near))
    def _():
        near[: SEG * (SLOTS - 1), :] = jnp.zeros((SEG * (SLOTS - 1), 2 * width), jnp.bfloat16)

    @pl.when(jnp.logical_not(has_far))
    def _():
        far[...] = jnp.zeros(far.shape, jnp.bfloat16)

    lane = lax.broadcasted_iota(jnp.int32, (SEG, width), 1)
    def pack_segments(index):
        for s in index:
            block = ya[pl.ds(pl.multiple_of((s + 1) * SEG, SEG), SEG), :].astype(jnp.float32)
            turned = pltpu.roll(block[:, width:], width // 2, 1)
            pack[pl.ds(pl.multiple_of(s * SEG, SEG), SEG), :] = jnp.where(
                lane < width // 2, block[:, :width], turned
            ).astype(jnp.bfloat16)

    def pack_extra(index):
        for e in index:
            total = jnp.zeros((SEG, width), jnp.float32)
            for g in range(PAD // EXTRA_ROWS):
                first = pl.multiple_of((e + 1) * SEG, SEG) + g * EXTRA_ROWS
                block = ya[pl.ds(first, SEG), :].astype(jnp.float32)
                for w in range(2):
                    place = (2 * g + w) * EXTRA
                    turned = pltpu.roll(
                        block[:, w * width : (w + 1) * width], (place + width // 2) % width, 1
                    )
                    total = jnp.where((lane >= place) & (lane < place + EXTRA), turned, total)
            extra[pl.ds(pl.multiple_of(e * SEG, SEG), SEG), :] = total.astype(jnp.bfloat16)

    def far_block(s):
        group, row = s // (EXTRA_ROWS // SEG), lax.rem(s, EXTRA_ROWS // SEG)
        first = far[0, pl.ds(pl.multiple_of(s * SEG, SEG), SEG), :].astype(jnp.float32)
        row = jnp.where(odd, row, s)
        rest = far[1, pl.ds(pl.multiple_of(row * SEG, SEG), SEG), :].astype(jnp.float32)
        half = width // 2
        both = []
        for w in range(2):
            body = first if w == 0 else pltpu.roll(first, half, 1)
            turn = lax.rem(half + width - (2 * group + w) * EXTRA, width)
            both.append(jnp.where(lane < half, body, pltpu.roll(rest, turn, 1)))
        block = jnp.concatenate(
            [jnp.where(odd, both[0], first), jnp.where(odd, both[1], rest)], 1
        )
        return block.astype(jnp.bfloat16)

    def spread(slot, s, spec):
        at = slot * SECOND + s
        bins[pl.ds(at, 2 * BINS, stride=BIN_PITCH), :] = spec[:, :width]
        bins[pl.ds(at + SLOTS, 2 * BINS, stride=BIN_PITCH), :] = spec[:, width:]

    def long_segments(index):
        specs = []
        for s in index:
            block = ya[s * SEG : s * SEG + SPAN, :]
            specs.append(jnp.dot(fa[...], block, preferred_element_type=jnp.float32))
        for s, spec in zip(index, specs):
            spread(1, s, spec)

    def short_batch(block_of, slot, absent, index):
        specs = []
        for s in index:
            block = block_of(s)
            twice = jnp.concatenate([block, block], 0)
            if isinstance(s, int):
                kind = 0 if s < FULL else 2 if s == FULL else 1
            else:
                kind = jnp.where(s < FULL, 0, jnp.where(s == FULL, 2, 1))
            if absent is not None:
                kind = jnp.where(absent, 1, kind)
            specs.append(jnp.dot(fd[kind], twice, preferred_element_type=jnp.float32))
        for s, spec in zip(index, specs):
            spread(slot, s, spec)

    def short_segments(block_of, slot, absent):
        unrolled(SLOTS, functools.partial(short_batch, block_of, slot, absent), 8)

    def place_of(s):
        return s * SEG if isinstance(s, int) else pl.multiple_of(s * SEG, SEG)

    def own_block(s):
        return ya[pl.ds(place_of(s + 1), SEG), :]

    def near_block(s):
        return near[pl.ds(place_of(s), SEG), :]

    def of_bin(slot, b):
        first = b * 2 * BIN_PITCH + slot * SECOND
        return bins[pl.ds(first, 2 * SLOTS), :], bins[pl.ds(first + BIN_PITCH, 2 * SLOTS), :]

    def product(slot, b, first):
        real, imag = [part.astype(jnp.bfloat16) for part in of_bin(slot, b)]
        both = jnp.concatenate(
            [jnp.concatenate([real, imag], 0), jnp.concatenate([-imag, real], 0)], 1
        )
        return jnp.dot(sega[b, first:, :], both, preferred_element_type=jnp.float32)

    def keep(target, pitch, b, cross):
        first = b * 2 * pitch
        target[pl.ds(first, width), :] = cross[:, :width]
        target[pl.ds(first + pitch, width), :] = cross[:, width:]

    def gram_next(index):
        for b, cross in zip(index, [product(1, b, 0) for b in index]):
            keep(gram, NEXT_PITCH, b, cross)

    def gram_own(index):
        for b in index:
            sega[b] = jnp.concatenate(of_bin(1, b), 0).astype(jnp.bfloat16).T
        for b, cross in zip(index, [product(0, b, 0) for b in index]):
            keep(bins, BIN_PITCH, b, cross)

    tall = width - NO_FAR
    same = lax.broadcasted_iota(jnp.int32, (tall, width), 1)
    same = same > lax.broadcasted_iota(jnp.int32, (tall, width), 0) + NO_FAR

    def gram_far(index):
        crosses = [product(1, b, NO_FAR) for b in index]
        places = [pl.ds((2 * b + h) * BIN_PITCH + NO_FAR, tall) for b in index for h in range(2)]
        before = [bins[place, :] for place in places]
        for e, place in enumerate(places):
            h = e % 2
            cross = crosses[e // 2][:, h * width : (h + 1) * width]
            bins[place, :] = jnp.where(same, before[e], cross)

    def place_next(ahead, c):
        return width + ahead - c

    def place_own(ahead, c):
        return jnp.where(ahead + 7 > c, ahead - c, 2 * width + ahead - c)

    def lag_step(source, pitch, place, base):
        def step(index):
            cross = jnp.concatenate(
                [
                    source[pl.ds(base + c, 2 * BINS, stride=pitch), :].astype(jnp.bfloat16)
                    for c in index
                ],
                1,
            )
            lags = lax.dot_general(
                cross, lag[...], (((0,), (0,)), ((), ())), preferred_element_type=jnp.float32
            )
            for u, c in enumerate(index):
                for e in range(width // 8):
                    k = jnp.clip(place(8 * e, base + c), -FIRST, BAND + 1)
                    at = u * width + 8 * e
                    first = (k + FIRST) * ROW_PITCH + c
                    rows[pl.ds(first, 8, stride=ROW_PITCH), :] = lags[at : at + 8]

        return step

    done = MID
    for c in range(PIECES):
        tables[c].wait()
        halves = []
        for parity in range(2):
            total = jnp.zeros((piece, 2 * width), jnp.float32)
            for p in range(parity * KEPT // 128, (parity + 1) * KEPT // 128, 2):
                first = c % 2 * area + p * piece
                block = jnp.concatenate(
                    [part[first : first + piece, :], part[first + piece : first + 2 * piece, :]], 1
                )
                total += jnp.dot(
                    block, white[p * 128 : (p + 2) * 128, :], preferred_element_type=jnp.float32
                )
            halves.append(total)
        if c + 2 < PIECES:
            tables[c + 2].start()
        first, end = c * piece, (c + 1) * piece
        kept = min(end, MID) - first
        ya[first : first + kept, :] = (halves[0] + halves[1])[:kept].astype(jnp.bfloat16)
        later = halves[0] - halves[1]
        for w in range(2):
            rows[w * BASE + first : w * BASE + end, :] = later[:, w * width : (w + 1) * width]
        ready = (end + SAMP // 2) // 16 * 16
        for w in range(2):
            source = slice(w * BASE + done - SAMP // 2, w * BASE + ready - SAMP // 2)
            ya[done:ready, w * width : (w + 1) * width] = rows[source, :].astype(jnp.bfloat16)
        done = ready
        if c == PIECES - 1:
            ya[done:, :] = jnp.zeros((SERIES - done, 2 * width), jnp.bfloat16)
        if c == 0:
            pl.semaphore_wait(barrier, len(peers))

        @pl.when(j > 0)
        def _():
            for h in range(2):
                to_near[2 * c + h].start()

        long_segments(turns_long[c])
        short_batch(own_block, 0, None, turns_short[c])

    unrolled(BINS, gram_own, 8)

    @pl.when(odd)
    def _():
        unrolled(SLOTS, pack_segments, 16)
        unrolled(EXTRA_ROWS // SEG, pack_extra, 6)

    for c in range(PIECES):

        @pl.when(has_near)
        def _():
            for h in range(2):
                to_near[2 * c + h].wait_recv()

        if c == PIECES - 1:

            @pl.when(odd & (j > 1))
            def _():
                for copy in to_far:
                    copy.start()

        short_batch(near_block, 1, j == blocks - 1, turns_short[c])

    @pl.when(odd & has_near)
    def _():
        for copy in pass_on:
            copy.start()

    unrolled(BINS, gram_next, 8)

    def take_far():
        @pl.when(odd & has_far)
        def _():
            for copy in to_far:
                copy.wait_recv()

        @pl.when(jnp.logical_not(odd) & has_far)
        def _():
            for copy in pass_on:
                copy.wait_recv()

        short_segments(far_block, 1, j >= blocks - 2)
        unrolled(BINS, gram_far, 8)

    def at(column, row):
        return row * RING + lax.rem(column + RING, RING)

    half = share // 2 + 1
    low, high, whole = (0, half), (half, share - half), (0, share)

    def spot(n, place, k, per):
        return pl.multiple_of(((n * per + place) * share + k) * CHUNK, CHUNK)

    def part_at(n, place, k=0, count=1):
        return pl.ds(spot(n, place, k, BAND // share), count * CHUNK)

    def inbox_at(n, place, k=0, count=1):
        return pl.ds(spot(n, place, k, BOXES), count * CHUNK)

    def message(n, m):
        def block(column, row, ks):
            return part.at[part_at(n, at(column, row), *ks)]

        def box(place, ks):
            return inbox.at[inbox_at(n, place, *ks)]

        if KINDS[n] == "X":
            source, target, device = [
                (block(x + 2, 0, whole), box(0, whole), right),
                (block(x + 2, 1, whole), box(1, whole), left),
                (block(x + 1, 1, whole), box(3, whole), right),
                (block(x - 1, 0, whole), box(4, whole), left),
                (block(x + 1, 0, whole), box(2, whole), right),
                (block(x - 1, 1, whole), box(5, whole), left),
                (block(x, 1 - z, whole), box(6, whole), other),
            ][m]
        else:
            four = (0, RING * share)
            source, target, device = [
                (part.at[part_at(n, (1 - z) * RING, *four)], box(0, four), other),
                (block(x + 2, z, low), box(4, low), right),
                (block(x + 2, z, high), box(4, high), left),
                (block(x + 1, z, high), box(5, high), right),
                (block(x - 1, z, low), box(6, low), left),
                (block(x + 1, z, low), box(5, low), right),
                (block(x - 1, z, high), box(6, high), left),
            ][m]
        return remote(source, target, sent.at[n, m], come.at[n, m], device)

    def start(n, *which):
        for m in which:
            message(n, m).start()

    def wait(n, *which):
        for m in which:
            message(n, m).wait_recv()

    def summed(n, place, boxes, k):
        total = part[part_at(n, place, k), :].astype(jnp.float32)
        for box in boxes:
            total += inbox[inbox_at(n, box, k), :].astype(jnp.float32)
        return total

    def plus(n, place, boxes, ks):
        first, count = ks

        def step(index):
            for k in index:
                total = summed(n, place, boxes, first + k)
                part[part_at(n, place, first + k), :] = total.astype(jnp.bfloat16)

        unrolled(count, step, 5 if count % 5 == 0 else count)

    def begin(n):
        unrolled(CHUNK, lag_step(gram, NEXT_PITCH, place_next, n * CHUNK), 8)
        unrolled(CHUNK, lag_step(bins, BIN_PITCH, place_own, n * CHUNK), 8)

        def step(index):
            for k in index:
                for d in range(BAND // share):
                    first = (d * share + k + FIRST + 1) * ROW_PITCH
                    part[part_at(n, d, k), :] = rows[pl.ds(first, CHUNK), :].astype(jnp.bfloat16)

        unrolled(share, step, 5)
        start(n, *((0, 1, 2, 3) if KINDS[n] == "X" else (0,)))

    def second(n):
        if KINDS[n] == "X":
            wait(n, 0, 1)
            plus(n, at(x + 1, 0), [0], whole)
            start(n, 4)
            plus(n, at(x - 1, 1), [1], whole)
            start(n, 5)
        else:
            wait(n, 0)
            for step in (2, 1, 3, 0):
                plus(n, at(x + step, z), [(x + step) % RING], whole)
                start(n, *{2: (1, 2), 1: (3,), 3: (4,), 0: ()}[step])

    def third(n):
        if KINDS[n] == "X":
            wait(n, 2, 3, 4, 5)
            plus(n, at(x, 1 - z), [3 - z, 5 - z], whole)
            start(n, 6)
        else:
            wait(n, 1, 2)
            plus(n, at(x + 1, z), [4], low)
            start(n, 5)
            plus(n, at(x - 1, z), [4], high)
            start(n, 6)

    def last(n):
        if KINDS[n] == "X":
            wait(n, 6)
            boxes = (2 + z, 4 + z, 6)
        else:
            wait(n, 3, 4, 5, 6)
            boxes = (5, 6)

        slot = n % 2
        if n in shown:
            shown[n].wait()

        def step(index):
            for k in index:
                stage[slot, k] = summed(n, at(x, z), boxes, k)

        unrolled(share, step, 5)
        result(n).start()
        for m in range(7):
            message(n, m).wait_send()

    def result(n):
        return pltpu.make_async_copy(
            stage.at[n % 2], out.at[:, pl.ds(n * CHUNK, CHUNK)], local.at[2 + n % 2]
        )

    order = [int(name[1:]) for name in STEPS if name[0] == "l"]
    shown, ending = {}, {}
    for n in order:
        if n % 2 in ending:
            shown[n] = result(ending[n % 2])
        ending[n % 2] = n
    stages = {"b": begin, "s": second, "t": third, "l": last}
    for name in STEPS:
        if name == "f":
            take_far()
        else:
            stages[name[0]](int(name[1:]))

    for n in ending.values():
        result(n).wait()

    @pl.when(j > 0)
    def _():
        for copy in to_near:
            copy.wait_send()

    @pl.when(odd & (j > 1))
    def _():
        for copy in to_far:
            copy.wait_send()

    @pl.when(odd & has_near)
    def _():
        for copy in pass_on:
            copy.wait_send()


def correlate(white, windows, groups):
    width = white.shape[1] // 2
    share = BAND // groups
    chunks = width // CHUNK
    fa, fd = segment_tables()
    vmem = pl.BlockSpec(memory_space=pltpu.VMEM)
    hbm = pl.BlockSpec(memory_space=pl.ANY)
    block = share * CHUNK
    return pl.pallas_call(
        pair_kernel,
        out_shape=jax.ShapeDtypeStruct((share, width, LAGS), jnp.float32),
        in_specs=[vmem, hbm, vmem, vmem, vmem],
        out_specs=hbm,
        scratch_shapes=[
            pltpu.VMEM((BINS, width, HELD), jnp.bfloat16),
            pltpu.VMEM((2 * BINS * BIN_PITCH, width), jnp.float32),
            pltpu.VMEM((2 * BINS * NEXT_PITCH, width), jnp.float32),
            pltpu.VMEM((OUT_ROWS * ROW_PITCH, LAGS), jnp.float32),
            pltpu.VMEM((SERIES, 2 * width), jnp.bfloat16),
            pltpu.VMEM((PAD, 2 * width), jnp.bfloat16),
            pltpu.VMEM((PAD, width), jnp.bfloat16),
            pltpu.VMEM((EXTRA_ROWS, width), jnp.bfloat16),
            pltpu.VMEM((2, PAD, width), jnp.bfloat16),
            pltpu.VMEM((chunks * groups * block, LAGS), jnp.bfloat16),
            pltpu.VMEM((chunks * BOXES * block, LAGS), jnp.bfloat16),
            pltpu.VMEM((2, share, CHUNK, LAGS), jnp.float32),
            pltpu.SemaphoreType.DMA((chunks, 7)),
            pltpu.SemaphoreType.DMA((chunks, 7)),
            pltpu.SemaphoreType.DMA((2 * PIECES + 4,)),
            pltpu.SemaphoreType.DMA((2 * PIECES + 2,)),
            pltpu.SemaphoreType.DMA((4,)),
        ],
        compiler_params=pltpu.CompilerParams(
            vmem_limit_bytes=63 * 2**20, collective_id=0, has_side_effects=True
        ),
        cost_estimate=pl.CostEstimate(flops=6 * 10**9, bytes_accessed=24 * 10**6, transcendentals=0),
    )(
        white,
        jnp.asarray(inverse_table()),
        jnp.asarray(fa),
        jnp.asarray(fd),
        jnp.asarray(lag_table(windows)),
    )


def body(record, starts):
    groups = lax.axis_size("tm")
    white = whitened(record, starts)
    return correlate(white, starts.shape[0] * groups, groups)


def solution(mesh):
    return jax.shard_map(
        body,
        mesh=mesh,
        in_specs=(P("tm", "chan"), P("tm")),
        out_specs=P("tm", "chan", None),
        check_vma=False,
    )
```
